32 devices in a mesh: tm: 8 (over z, core), head: 4 (over y, x).
Axes of the slice: x: 2, y: 2, z: 4, core: 2. Of those that a mesh axis runs over, the one named last changes fastest.
Arguments:
- frames: bfloat16 [4096, 2048], P(('tm', 'head')), may hold values from -6 to 6
- log_decay: float32 [4096, 16], P('tm', 'head'), may hold values from -2 to 0, as said below
- w_query: bfloat16 [2048, 2048], P('tm', 'head'), may hold values from -0.125 to 0.125
- w_key: bfloat16 [2048, 2048], P('tm', 'head'), may hold values from -0.125 to 0.125
- w_value: bfloat16 [2048, 2048], P('tm', 'head'), may hold values from -0.125 to 0.125
- w_gate: bfloat16 [2048, 2048], P('tm', 'head'), may hold values from -0.125 to 0.125
- w_out: bfloat16 [2048, 2048], P('head', 'tm'), may hold values from -0.125 to 0.125
Outputs:
- mixed: bfloat16 [4096, 2048], P(('tm', 'head'))
The draws below stay inside these ranges and needn't reach their ends.
Inputs may be any that keep to these rules, and one draw needn't show every extreme that they name: `log_decay`: strictly negative.
All inputs are finite; a program needn't handle non-finite values.
Results may differ from the reference program's by a relative error of at most 0.015.
Values may be sent and summed in bfloat16 or wider, within the bound.
A program may use at most 64 MiB of HBM per device.

```python
import jax
import jax.numpy as jnp
from jax import lax

MEMORY_GROUPS = 16
HEAD_DIM = 128
D = 2048
BLOCK = 512
TOK_DEV = 512
AUDIO_SLICES = 4096


def draw_log_decay(key, part):
    noise_seed_collection = jax.random.split(key, 7)
    quick_share = 0.5
    quick_heads = jax.random.uniform(noise_seed_collection[0], (MEMORY_GROUPS,)) < quick_share
    slow_rate = 2.302585 / AUDIO_SLICES * jax.random.uniform(noise_seed_collection[1], (MEMORY_GROUPS,), minval=0.1, maxval=0.25)
    quick_rate = 1.0 / jax.random.uniform(noise_seed_collection[2], (MEMORY_GROUPS,), minval=30.0, maxval=50.0)
    floor_decay_speed = jnp.where(quick_heads, quick_rate, slow_rate)
    span_count = AUDIO_SLICES // TOK_DEV
    width_factor = jnp.exp(jax.random.uniform(noise_seed_collection[3], (span_count, MEMORY_GROUPS), minval=-0.693, maxval=0.693))
    width_factor = jnp.repeat(width_factor, TOK_DEV, axis=0)
    noise_jitter = jax.random.uniform(noise_seed_collection[4], (AUDIO_SLICES, MEMORY_GROUPS), minval=0.3, maxval=1.7)
    slices_within_segment = jax.random.randint(noise_seed_collection[5], (2, MEMORY_GROUPS), 0, AUDIO_SLICES)
    segment_damping = jnp.log(jax.random.uniform(noise_seed_collection[6], (2, MEMORY_GROUPS), minval=0.5, maxval=0.8))
    slice_ordinal = jnp.arange(AUDIO_SLICES, dtype=jnp.int32)[:, None]
    segment_collection = jnp.where(slice_ordinal == slices_within_segment[0][None, :], segment_damping[0][None, :], 0.0)
    segment_collection = segment_collection + jnp.where(slice_ordinal == slices_within_segment[1][None, :], segment_damping[1][None, :], 0.0)
    return (-floor_decay_speed[None, :] * width_factor * noise_jitter + segment_collection).astype(jnp.float32)


def levels(rng, shape, pieces, low, top_value):
    level = 1.0
    for axis_at, shards_of in pieces:
        steps = jax.random.uniform(jax.random.fold_in(jax.random.fold_in(rng, 6), axis_at), (shards_of,), jnp.float32, low / len(pieces), top_value / len(pieces))
        level = level * jnp.repeat(jnp.exp(steps), shape[axis_at] // shards_of).reshape((-1,) + (1,) * (len(shape) - 1 - axis_at))
    return level


def noise(stream_key, shape, width, limit, cuts=(), kind=jnp.bfloat16):
    entries = width * jax.random.normal(stream_key, shape, jnp.float32)
    if cuts:
        entries = entries * levels(stream_key, shape, cuts, -0.22, 0.18)
    return jnp.clip(entries, -limit, limit).astype(kind)


def setup_inputs(seed: int = 0) -> dict:
    key_list = jax.random.split(jax.random.key(seed), 8)
    return {
        "frames": noise(key_list[0], (AUDIO_SLICES, D), 1.0, 6.0, ((0, 32),)),
        "log_decay": draw_log_decay(jax.random.fold_in(key_list[7], 71), 0),
        "w_query": noise(key_list[2], (D, D), D ** -0.5, 0.125, ((0, 8), (1, 4))),
        "w_key": noise(key_list[3], (D, D), D ** -0.5, 0.125, ((0, 8), (1, 4))),
        "w_value": noise(key_list[4], (D, D), D ** -0.5, 0.125, ((0, 8), (1, 4))),
        "w_gate": noise(key_list[5], (D, D), D ** -0.5, 0.125, ((0, 8), (1, 4))),
        "w_out": noise(key_list[6], (D, D), D ** -0.5, 0.125, ((0, 4), (1, 8))),
    }


def reference(frames, log_decay, w_query, w_key, w_value, w_gate, w_out):
    query_all = jnp.dot(frames, w_query, preferred_element_type=jnp.float32).astype(jnp.bfloat16)
    key_all = jnp.dot(frames, w_key, preferred_element_type=jnp.float32).astype(jnp.bfloat16)
    value_all = jnp.dot(frames, w_value, preferred_element_type=jnp.float32).astype(jnp.bfloat16)
    gate_all = jnp.dot(frames, w_gate, preferred_element_type=jnp.float32)
    block_count = AUDIO_SLICES // BLOCK
    query_blocks = query_all.reshape(block_count, BLOCK, MEMORY_GROUPS, HEAD_DIM)
    key_blocks = key_all.reshape(block_count, BLOCK, MEMORY_GROUPS, HEAD_DIM)
    value_blocks = value_all.reshape(block_count, BLOCK, MEMORY_GROUPS, HEAD_DIM)
    decay_blocks = log_decay.reshape(block_count, BLOCK, MEMORY_GROUPS)
    slice_ordinal = jnp.arange(BLOCK, dtype=jnp.int32)
    causal = slice_ordinal[:, None] >= slice_ordinal[None, :]

    def advance(carry_state, inputs):
        query_block, key_block, value_block, decay_block = inputs
        running = jnp.cumsum(decay_block, axis=0)
        gaps = running.T[:, :, None] - running.T[:, None, :]
        decay = jnp.exp(jnp.where(causal[None], gaps, -jnp.inf))
        scores = jnp.einsum('thd,shd->hts', query_block.astype(jnp.float32), key_block.astype(jnp.float32))
        weights = (scores * decay).astype(jnp.bfloat16)
        intra = jnp.einsum('hts,shd->thd', weights.astype(jnp.float32), value_block.astype(jnp.float32))
        lifted = query_block.astype(jnp.float32) * jnp.exp(running)[:, :, None]
        inter = jnp.einsum('thd,hde->the', lifted, carry_state, precision=lax.Precision.HIGHEST)
        scaled = (key_block.astype(jnp.float32) * jnp.exp(running[-1][None, :] - running)[:, :, None]).astype(jnp.bfloat16)
        update = jnp.einsum('shd,she->hde', scaled.astype(jnp.float32), value_block.astype(jnp.float32))
        next_state = jnp.exp(running[-1])[:, None, None] * carry_state + update
        return (next_state, intra + inter)
    start_state = jnp.zeros((MEMORY_GROUPS, HEAD_DIM, HEAD_DIM), jnp.float32)
    _, retained = lax.scan(advance, start_state, (query_blocks, key_blocks, value_blocks, decay_blocks))
    retained = retained.reshape(AUDIO_SLICES, MEMORY_GROUPS, HEAD_DIM)
    center = lax.optimization_barrier(jnp.mean(retained, axis=-1, keepdims=True))
    spread = lax.optimization_barrier(jnp.mean((retained - center) ** 2, axis=-1, keepdims=True))
    normed = (retained - center) / jnp.sqrt(spread + 1e-05)
    gated = (jax.nn.silu(gate_all.reshape(AUDIO_SLICES, MEMORY_GROUPS, HEAD_DIM)) * normed).astype(jnp.bfloat16).reshape(AUDIO_SLICES, D)
    return jnp.dot(gated, w_out, preferred_element_type=jnp.float32).astype(jnp.bfloat16)
```

```python
import functools

import jax
import jax.numpy as jnp
from jax import lax
from jax.experimental import pallas as pl
from jax.experimental.pallas import tpu as pltpu
from jax.sharding import PartitionSpec as P

HEAD_DIM = 128
MESH = pl.DeviceIdType.MESH
F32 = jnp.float32
BF16 = jnp.bfloat16


def kernel(
    tms, heads_axis, x_ref, ld_ref, wk_ref, wv_ref, wq_ref, wg_ref, wo_ref, out_ref,
    x, w, wo, acc, decay, runs, sown, sprev, rin, rout, ret, gated, owned,
    x_send, x_recv, w_send, w_recv, o_recv, oxy_send, osib_send,
    s_send, s_recv, r_send, r_recv, rs_send, g_send, g_recv,
):
    zs = tms // 2
    tm, hd = lax.axis_index("tm"), lax.axis_index("head")
    z, c = lax.div(tm, 2), lax.rem(tm, 2)
    sibling = (2 * z + 1 - c, hd)
    rows = wk_ref.shape[0]
    width = wk_ref.shape[1]
    frames_here = x_ref.shape[0]
    length = frames_here * heads_axis
    heads = width // HEAD_DIM

    def peer(p):
        return lax.rem(hd + p, heads_axis)

    def remote(ref_from, ref_to, send, recv, device):
        return pltpu.make_async_remote_copy(
            src_ref=ref_from, dst_ref=ref_to, send_sem=send, recv_sem=recv,
            device_id=device, device_id_type=MESH,
        )

    def slot(m, position):
        if m == 0:
            return wo.at[hd, position], o_recv.at[hd, position]
        return w.at[m - 1, position], w_recv.at[m - 1, position]

    def along(m, zo, side):
        ref, recv = slot(m, 2 * zo + c)
        to = z + 1 - 2 * side
        return remote(ref, ref, w_send.at[m, zo, side], recv, (2 * to + c, hd))

    def across(m, zo):
        ref, recv = slot(m, 2 * zo + c)
        return remote(ref, ref, w_send.at[m, zo, 2], recv, sibling)

    def landed(m, position):
        ref, recv = slot(m, position)
        remote(ref, ref, w_send.at[m, 0, 2], recv, sibling).wait_recv()

    def plane(zo, p):
        ref = wo.at[hd, 2 * zo + c]
        return remote(ref, ref, oxy_send.at[zo, p], o_recv.at[hd, 2 * zo + c], (tm, peer(p)))

    def plane_across(zo, p):
        at = peer(p)
        ref = wo.at[at, 2 * zo + c]
        return remote(ref, ref, osib_send.at[zo, p], o_recv.at[at, 2 * zo + c], sibling)

    def out_landed(at, position):
        ref = wo.at[at, position]
        remote(ref, ref, osib_send.at[0, 0], o_recv.at[at, position], sibling).wait_recv()

    def both(d, body):
        def one(side, _):
            zo = z - d + 2 * d * side
            first = jnp.logical_or(side == 0, d > 0)

            @pl.when(jnp.logical_and(first, jnp.logical_and(zo >= 0, zo < zs)))
            def _():
                body(zo, side)

            return 0

        lax.fori_loop(0, 2, one, 0)

    def pass_on(m, d):
        def body(zo, side):
            landed(m, 2 * zo + c)
            to = z + 1 - 2 * side

            @pl.when(jnp.logical_and(to >= 0, to < zs))
            def _():
                along(m, zo, side).start()

            across(m, zo).start()
            if m == 0:
                for p in range(1, heads_axis):
                    plane(zo, p).start()

        both(d, body)

    def project(m, d):
        def body(zo, side):
            landed(m, 2 * zo + 1 - c)
            columns = pl.ds(pl.multiple_of(zo * (2 * rows), 2 * rows), 2 * rows)
            block = w[m - 1, pl.ds(2 * zo, 2)].reshape(2 * rows, width)
            acc[m - 1] += jnp.dot(x[:, columns], block, preferred_element_type=F32)

        both(d, body)

    def plane_pass_on(d):
        def body(zo, side):
            for p in range(1, heads_axis):
                out_landed(peer(p), 2 * zo + c)
                plane_across(zo, p).start()

        both(d, body)

    barrier = pltpu.get_barrier_semaphore()
    pl.semaphore_signal(barrier, inc=1, device_id=sibling, device_id_type=MESH)
    for p in range(1, heads_axis):
        pl.semaphore_signal(barrier, inc=1, device_id=(tm, peer(p)), device_id_type=MESH)

    @pl.when(z > 0)
    def _():
        pl.semaphore_signal(barrier, inc=1, device_id=(tm - 2, hd), device_id_type=MESH)

    @pl.when(z < zs - 1)
    def _():
        pl.semaphore_signal(barrier, inc=1, device_id=(tm + 2, hd), device_id_type=MESH)

    here = pl.ds(pl.multiple_of(hd * frames_here, frames_here), frames_here)
    x[here, :] = x_ref[...]
    wo[hd, tm] = wo_ref[...]
    for m, ref in enumerate((wk_ref, wv_ref, wq_ref, wg_ref)):
        w[m, tm] = ref[...]
    neighbours = (z > 0).astype(jnp.int32) + (z < zs - 1).astype(jnp.int32)
    pl.semaphore_wait(barrier, heads_axis + neighbours)

    def x_copy(p):
        return remote(x.at[here, :], x.at[here, :], x_send.at[p], x_recv.at[hd], (tm, peer(p)))

    for p in range(1, heads_axis):
        x_copy(p).start()
    for m in range(5):

        @pl.when(z < zs - 1)
        def _():
            along(m, z, 0).start()

        @pl.when(z > 0)
        def _():
            along(m, z, 1).start()

        across(m, z).start()
        if m == 0:
            for p in range(1, heads_axis):
                plane(z, p).start()

    acc[...] = jnp.zeros_like(acc)
    at_row = lax.broadcasted_iota(jnp.int32, (length, length), 0)
    at_col = lax.broadcasted_iota(jnp.int32, (length, length), 1)
    for h in range(heads):
        steps = ld_ref[:, h : h + 1]
        run_row = jnp.sum(jnp.where(at_row <= at_col, steps, 0.0), axis=0, keepdims=True)
        run_col = jnp.sum(jnp.where(at_row == at_col, run_row, 0.0), axis=1, keepdims=True)
        runs[h] = jnp.broadcast_to(run_col, (length, HEAD_DIM))
        decay[h] = jnp.exp(jnp.where(at_row >= at_col, run_col - run_row, -jnp.inf))
    for p in range(1, heads_axis):
        at = peer(p)
        ref = x.at[pl.ds(pl.multiple_of(at * frames_here, frames_here), frames_here), :]
        remote(ref, ref, x_send.at[p], x_recv.at[at], sibling).wait_recv()

    def lap(d, _):
        for m in range(5):
            pass_on(m, d)
            if m > 0:
                project(m, d - 1)
        plane_pass_on(d - 1)
        return 0

    lax.fori_loop(1, zs - 1, lap, 0)
    for m in range(3):
        pass_on(m, zs - 1)
        if m > 0:
            project(m, zs - 2)
            project(m, zs - 1)

    def columns_of(h):
        return slice(h * HEAD_DIM, (h + 1) * HEAD_DIM)

    def first_copy(h):
        return remote(sown.at[h], sprev.at[h], s_send.at[h], s_recv.at[h], sibling)

    def next_copy(h):
        return remote(rout.at[h], rin.at[h], r_send.at[h], r_recv.at[h], (tm + 2, hd))

    def share_copy(h):
        return remote(rin.at[h], rin.at[h], rs_send.at[h], r_recv.at[h], sibling)

    def state_step(h):
        prior = jnp.exp(sprev[h, HEAD_DIM : HEAD_DIM + 1, :]) * rin[h] + sprev[h, :HEAD_DIM, :]
        rout[h] = jnp.exp(sown[h, HEAD_DIM : HEAD_DIM + 1, :]) * prior + sown[h, :HEAD_DIM, :]
        return prior

    @pl.when(z == 0)
    def _():
        rin[...] = jnp.zeros_like(rin)

    for h in range(heads):
        run = runs[h]
        last = run[length - 1 :, :]
        key = acc[0, :, columns_of(h)].astype(BF16)
        value = acc[1, :, columns_of(h)].astype(BF16)
        scaled = (key.astype(F32) * jnp.exp(last - run)).astype(BF16)
        sown[h, :HEAD_DIM, :] = lax.dot_general(
            scaled, value, (((0,), (0,)), ((), ())), preferred_element_type=F32
        )
        sown[h, HEAD_DIM:, :] = jnp.broadcast_to(last, (8, HEAD_DIM))

        @pl.when(c == 0)
        def _():
            first_copy(h).start()

    @pl.when(jnp.logical_and(c == 1, z == 0))
    def _():
        for h in range(heads):
            first_copy(h).wait_recv()
            state_step(h)
            next_copy(h).start()

    pass_on(3, zs - 1)
    project(3, zs - 2)
    project(3, zs - 1)
    for h in range(heads):
        query = acc[2, :, columns_of(h)].astype(BF16)
        key = acc[0, :, columns_of(h)].astype(BF16)
        value = acc[1, :, columns_of(h)].astype(BF16)
        scores = lax.dot_general(query, key, (((1,), (1,)), ((), ())), preferred_element_type=F32)
        weights = (scores * decay[h]).astype(BF16)
        ret[:, columns_of(h)] = jnp.dot(weights, value, preferred_element_type=F32)
    plane_pass_on(zs - 2)
    pass_on(4, zs - 1)
    project(4, zs - 2)

    @pl.when(jnp.logical_and(c == 1, z > 0))
    def _():
        for h in range(heads):
            first_copy(h).wait_recv()
        for h in range(heads):
            next_copy(h).wait_recv()
            state_step(h)

            @pl.when(z < zs - 1)
            def _():
                next_copy(h).start()

            share_copy(h).start()

    @pl.when(jnp.logical_and(c == 0, z > 0))
    def _():
        for h in range(heads):
            share_copy(h).wait_recv()

    for h in range(heads):

        @pl.when(c == 1)
        def _():
            rout[heads + h] = (
                jnp.exp(sprev[h, HEAD_DIM : HEAD_DIM + 1, :]) * rin[h] + sprev[h, :HEAD_DIM, :]
            )

        @pl.when(c == 0)
        def _():
            rout[heads + h] = rin[h]

        query = acc[2, :, columns_of(h)].astype(BF16)
        lifted = query.astype(F32) * jnp.exp(runs[h])
        both_parts = ret[:, columns_of(h)] + jnp.dot(
            lifted, rout[heads + h], preferred_element_type=F32, precision=lax.Precision.HIGHEST
        )
        centred = both_parts - jnp.mean(both_parts, axis=1, keepdims=True)
        spread = jnp.mean(centred * centred, axis=1, keepdims=True)
        ret[:, columns_of(h)] = centred * lax.rsqrt(spread + 1e-05)

    project(4, zs - 1)

    def g_copy(p):
        at = peer(p)
        piece = gated.at[pl.ds(pl.multiple_of(at * frames_here, frames_here), frames_here), :]
        return remote(piece, owned.at[hd], g_send.at[p], g_recv.at[hd], (tm, at))

    def gate_rows(at):
        part = pl.ds(pl.multiple_of(at * frames_here, frames_here), frames_here)
        gate = acc[3, part, :]
        return (gate / (1.0 + jnp.exp(-gate)) * ret[part, :]).astype(BF16)

    for p in range(1, heads_axis):
        at = peer(p)
        part = pl.ds(pl.multiple_of(at * frames_here, frames_here), frames_here)
        gated[part, :] = gate_rows(at)
        g_copy(p).start()
    owned[hd] = gate_rows(hd)

    plane_pass_on(zs - 1)

    def all_out(zo, _):
        for at in range(heads_axis):
            out_landed(at, 2 * zo + 1 - c)
        return 0

    lax.fori_loop(0, zs, all_out, 0)
    for p in range(1, heads_axis):
        at = peer(p)
        remote(owned.at[at], owned.at[at], g_send.at[p], g_recv.at[at], sibling).wait_recv()

    wide = wo_ref.shape[1]

    def finish(t, _):
        total = jnp.zeros((frames_here, wide), F32)
        for at in range(heads_axis):
            total += jnp.dot(owned[at], wo[at, t], preferred_element_type=F32)
        out_ref[:, pl.ds(pl.multiple_of(t * wide, wide), wide)] = total.astype(BF16)
        return 0

    lax.fori_loop(0, tms, finish, 0)

    for p in range(1, heads_axis):
        x_copy(p).wait_send()
        g_copy(p).wait_send()

    @pl.when(c == 0)
    def _():
        for h in range(heads):
            first_copy(h).wait_send()

    @pl.when(c == 1)
    def _():
        for h in range(heads):

            @pl.when(z < zs - 1)
            def _():
                next_copy(h).wait_send()

            @pl.when(z > 0)
            def _():
                share_copy(h).wait_send()

    def drain(zo, _):
        for m in range(5):
            across(m, zo).wait_send()

            @pl.when(jnp.logical_and(zo <= z, z < zs - 1))
            def _():
                along(m, zo, 0).wait_send()

            @pl.when(jnp.logical_and(zo >= z, z > 0))
            def _():
                along(m, zo, 1).wait_send()

        for p in range(1, heads_axis):
            plane(zo, p).wait_send()
            plane_across(zo, p).wait_send()
        return 0

    lax.fori_loop(0, zs, drain, 0)


def solution(mesh):
    tms, heads_axis = mesh.shape["tm"], mesh.shape["head"]
    zs = tms // 2

    def shards(frames, log_decay, w_query, w_key, w_value, w_gate, w_out):
        here, model = frames.shape
        rows, width = w_query.shape
        length, heads = log_decay.shape
        vmem = pl.BlockSpec(memory_space=pltpu.VMEM)
        dma = pltpu.SemaphoreType.DMA
        return pl.pallas_call(
            functools.partial(kernel, tms, heads_axis),
            out_shape=jax.ShapeDtypeStruct((here, model), BF16),
            in_specs=[vmem] * 7,
            out_specs=vmem,
            scratch_shapes=[
                pltpu.VMEM((length, model), BF16),
                pltpu.VMEM((4, tms, rows, width), BF16),
                pltpu.VMEM((heads_axis, tms) + w_out.shape, BF16),
                pltpu.VMEM((4, length, width), F32),
                pltpu.VMEM((heads, length, length), F32),
                pltpu.VMEM((heads, length, HEAD_DIM), F32),
                pltpu.VMEM((heads, HEAD_DIM + 8, HEAD_DIM), F32),
                pltpu.VMEM((heads, HEAD_DIM + 8, HEAD_DIM), F32),
                pltpu.VMEM((heads, HEAD_DIM, HEAD_DIM), F32),
                pltpu.VMEM((2 * heads, HEAD_DIM, HEAD_DIM), F32),
                pltpu.VMEM((length, width), F32),
                pltpu.VMEM((length, width), BF16),
                pltpu.VMEM((heads_axis, here, width), BF16),
                dma((heads_axis,)),
                dma((heads_axis,)),
                dma((5, zs, 3)),
                dma((4, tms)),
                dma((heads_axis, tms)),
                dma((zs, heads_axis)),
                dma((zs, heads_axis)),
                dma((heads,)),
                dma((heads,)),
                dma((heads,)),
                dma((heads,)),
                dma((heads,)),
                dma((heads_axis,)),
                dma((heads_axis,)),
            ],
            compiler_params=pltpu.CompilerParams(
                collective_id=0, has_side_effects=True, vmem_limit_bytes=50 * 2**20
            ),
        )(frames, log_decay, w_key, w_value, w_query, w_gate, w_out)

    return jax.shard_map(
        shards,
        mesh=mesh,
        in_specs=(
            P(("tm", "head"), None),
            P("tm", "head"),
            P("tm", "head"),
            P("tm", "head"),
            P("tm", "head"),
            P("tm", "head"),
            P("head", "tm"),
        ),
        out_specs=P(("tm", "head"), None),
        check_vma=False,
    )
```

```python
import functools

import jax
import jax.numpy as jnp
from jax import lax
from jax.experimental import pallas as pl
from jax.experimental.pallas import tpu as pltpu
from jax.sharding import PartitionSpec as P

HEAD_DIM = 128
MESH = pl.DeviceIdType.MESH
F32 = jnp.float32
BF16 = jnp.bfloat16


def kernel(
    tms, heads_axis, x_ref, ld_ref, wk_ref, wv_ref, wq_ref, wg_ref, wo_ref, out_ref,
    in_sem, x, w, wo, acc, decay, runs, sown, sprev, rin, rout, ret, gated, owned,
    x_send, x_recv, w_send, w_recv, o_recv, oxy_send, osib_send,
    s_send, s_recv, r_send, r_recv, rs_send, g_send, g_recv,
):
    zs = tms // 2
    tm, hd = lax.axis_index("tm"), lax.axis_index("head")
    z, c = lax.div(tm, 2), lax.rem(tm, 2)
    sibling = (2 * z + 1 - c, hd)
    rows = wk_ref.shape[0]
    width = wk_ref.shape[1]
    frames_here = x_ref.shape[0]
    length = frames_here * heads_axis
    heads = width // HEAD_DIM

    def peer(p):
        return lax.rem(hd + p, heads_axis)

    def remote(ref_from, ref_to, send, recv, device):
        return pltpu.make_async_remote_copy(
            src_ref=ref_from, dst_ref=ref_to, send_sem=send, recv_sem=recv,
            device_id=device, device_id_type=MESH,
        )

    def slot(m, position):
        if m == 0:
            return wo.at[hd, position], o_recv.at[hd, position]
        return w.at[m - 1, position], w_recv.at[m - 1, position]

    def along(m, zo, side):
        ref, recv = slot(m, 2 * zo + c)
        to = z + 1 - 2 * side
        return remote(ref, ref, w_send.at[m, zo, side], recv, (2 * to + c, hd))

    def across(m, zo):
        ref, recv = slot(m, 2 * zo + c)
        return remote(ref, ref, w_send.at[m, zo, 2], recv, sibling)

    def landed(m, position):
        ref, recv = slot(m, position)
        remote(ref, ref, w_send.at[m, 0, 2], recv, sibling).wait_recv()

    def plane(zo, p):
        ref = wo.at[hd, 2 * zo + c]
        return remote(ref, ref, oxy_send.at[zo, p], o_recv.at[hd, 2 * zo + c], (tm, peer(p)))

    def plane_across(zo, p):
        at = peer(p)
        ref = wo.at[at, 2 * zo + c]
        return remote(ref, ref, osib_send.at[zo, p], o_recv.at[at, 2 * zo + c], sibling)

    def out_landed(at, position):
        ref = wo.at[at, position]
        remote(ref, ref, osib_send.at[0, 0], o_recv.at[at, position], sibling).wait_recv()

    def both(d, body):
        def one(side, _):
            zo = z - d + 2 * d * side
            first = jnp.logical_or(side == 0, d > 0)

            @pl.when(jnp.logical_and(first, jnp.logical_and(zo >= 0, zo < zs)))
            def _():
                body(zo, side)

            return 0

        lax.fori_loop(0, 2, one, 0)

    def pass_on(m, d):
        def body(zo, side):
            landed(m, 2 * zo + c)
            to = z + 1 - 2 * side

            @pl.when(jnp.logical_and(to >= 0, to < zs))
            def _():
                along(m, zo, side).start()

            across(m, zo).start()
            if m == 0:
                for p in range(1, heads_axis):
                    plane(zo, p).start()

        both(d, body)

    def project(m, d):
        def body(zo, side):
            landed(m, 2 * zo + 1 - c)
            columns = pl.ds(pl.multiple_of(zo * (2 * rows), 2 * rows), 2 * rows)
            block = w[m - 1, pl.ds(2 * zo, 2)].reshape(2 * rows, width)
            acc[m - 1] += jnp.dot(x[:, columns], block, preferred_element_type=F32)

        both(d, body)

    def plane_pass_on(d):
        def body(zo, side):
            for p in range(1, heads_axis):
                out_landed(peer(p), 2 * zo + c)
                plane_across(zo, p).start()

        both(d, body)

    barrier = pltpu.get_barrier_semaphore()
    pl.semaphore_signal(barrier, inc=1, device_id=sibling, device_id_type=MESH)
    for p in range(1, heads_axis):
        pl.semaphore_signal(barrier, inc=1, device_id=(tm, peer(p)), device_id_type=MESH)

    @pl.when(z > 0)
    def _():
        pl.semaphore_signal(barrier, inc=1, device_id=(tm - 2, hd), device_id_type=MESH)

    @pl.when(z < zs - 1)
    def _():
        pl.semaphore_signal(barrier, inc=1, device_id=(tm + 2, hd), device_id_type=MESH)

    here = pl.ds(pl.multiple_of(hd * frames_here, frames_here), frames_here)
    own = [
        pltpu.make_async_copy(wo_ref, wo.at[hd, tm], in_sem.at[0]),
        pltpu.make_async_copy(wk_ref, w.at[0, tm], in_sem.at[1]),
        pltpu.make_async_copy(wv_ref, w.at[1, tm], in_sem.at[2]),
        pltpu.make_async_copy(wq_ref, w.at[2, tm], in_sem.at[3]),
        pltpu.make_async_copy(wg_ref, w.at[3, tm], in_sem.at[4]),
        pltpu.make_async_copy(x_ref, x.at[here, :], in_sem.at[5]),
    ]
    for copy in own:
        copy.start()
    neighbours = (z > 0).astype(jnp.int32) + (z < zs - 1).astype(jnp.int32)
    pl.semaphore_wait(barrier, heads_axis + neighbours)

    def x_copy(p):
        return remote(x.at[here, :], x.at[here, :], x_send.at[p], x_recv.at[hd], (tm, peer(p)))

    for m in range(5):
        own[m].wait()

        @pl.when(z < zs - 1)
        def _():
            along(m, z, 0).start()

        @pl.when(z > 0)
        def _():
            along(m, z, 1).start()

        across(m, z).start()
        if m == 0:
            own[5].wait()
            for p in range(1, heads_axis):
                x_copy(p).start()
            for p in range(1, heads_axis):
                plane(z, p).start()

    acc[...] = jnp.zeros_like(acc)
    at_row = lax.broadcasted_iota(jnp.int32, (length, length), 0)
    at_col = lax.broadcasted_iota(jnp.int32, (length, length), 1)
    for h in range(heads):
        steps = ld_ref[:, h : h + 1]
        run_row = jnp.sum(jnp.where(at_row <= at_col, steps, 0.0), axis=0, keepdims=True)
        run_col = jnp.sum(jnp.where(at_row == at_col, run_row, 0.0), axis=1, keepdims=True)
        runs[h] = jnp.broadcast_to(run_col, (length, HEAD_DIM))
        decay[h] = jnp.exp(jnp.where(at_row >= at_col, run_col - run_row, -jnp.inf))
    def frames_landed():
        for p in range(1, heads_axis):
            at = peer(p)
            ref = x.at[pl.ds(pl.multiple_of(at * frames_here, frames_here), frames_here), :]
            remote(ref, ref, x_send.at[p], x_recv.at[at], sibling).wait_recv()

    def lap(d, _):
        for m in range(5):
            pass_on(m, d)

        @pl.when(d == 1)
        def _():
            frames_landed()

        for m in range(1, 5):
            project(m, d - 1)

        @pl.when(d > 1)
        def _():
            plane_pass_on(d - 2)

        return 0

    lax.fori_loop(1, zs - 1, lap, 0)
    for m in range(3):
        pass_on(m, zs - 1)
        if m > 0:
            project(m, zs - 2)
            project(m, zs - 1)

    def columns_of(h):
        return slice(h * HEAD_DIM, (h + 1) * HEAD_DIM)

    def first_copy(h):
        return remote(sown.at[h], sprev.at[h], s_send.at[h], s_recv.at[h], sibling)

    def next_copy(h):
        return remote(rout.at[h], rin.at[h], r_send.at[h], r_recv.at[h], (tm + 2, hd))

    def share_copy(h):
        return remote(rin.at[h], rin.at[h], rs_send.at[h], r_recv.at[h], sibling)

    def state_step(h):
        prior = jnp.exp(sprev[h, HEAD_DIM : HEAD_DIM + 1, :]) * rin[h] + sprev[h, :HEAD_DIM, :]
        rout[h] = jnp.exp(sown[h, HEAD_DIM : HEAD_DIM + 1, :]) * prior + sown[h, :HEAD_DIM, :]
        return prior

    @pl.when(z == 0)
    def _():
        rin[...] = jnp.zeros_like(rin)

    for h in range(heads):
        run = runs[h]
        last = run[length - 1 :, :]
        key = acc[0, :, columns_of(h)].astype(BF16)
        value = acc[1, :, columns_of(h)].astype(BF16)
        scaled = (key.astype(F32) * jnp.exp(last - run)).astype(BF16)
        sown[h, :HEAD_DIM, :] = lax.dot_general(
            scaled, value, (((0,), (0,)), ((), ())), preferred_element_type=F32
        )
        sown[h, HEAD_DIM:, :] = jnp.broadcast_to(last, (8, HEAD_DIM))

        @pl.when(c == 0)
        def _():
            first_copy(h).start()

    @pl.when(jnp.logical_and(c == 1, z == 0))
    def _():
        for h in range(heads):
            first_copy(h).wait_recv()
            state_step(h)
            next_copy(h).start()

    pass_on(3, zs - 1)
    project(3, zs - 2)
    project(3, zs - 1)
    for h in range(heads):
        query = acc[2, :, columns_of(h)].astype(BF16)
        key = acc[0, :, columns_of(h)].astype(BF16)
        value = acc[1, :, columns_of(h)].astype(BF16)
        scores = lax.dot_general(query, key, (((1,), (1,)), ((), ())), preferred_element_type=F32)
        weights = (scores * decay[h]).astype(BF16)
        ret[:, columns_of(h)] = jnp.dot(weights, value, preferred_element_type=F32)
    pass_on(4, zs - 1)
    plane_pass_on(zs - 3)
    plane_pass_on(zs - 2)
    project(4, zs - 2)

    @pl.when(jnp.logical_and(c == 1, z > 0))
    def _():
        for h in range(heads):
            first_copy(h).wait_recv()
        for h in range(heads):
            next_copy(h).wait_recv()
            state_step(h)

            @pl.when(z < zs - 1)
            def _():
                next_copy(h).start()

            share_copy(h).start()

    @pl.when(jnp.logical_and(c == 0, z > 0))
    def _():
        for h in range(heads):
            share_copy(h).wait_recv()

    for h in range(heads):

        @pl.when(c == 1)
        def _():
            rout[heads + h] = (
                jnp.exp(sprev[h, HEAD_DIM : HEAD_DIM + 1, :]) * rin[h] + sprev[h, :HEAD_DIM, :]
            )

        @pl.when(c == 0)
        def _():
            rout[heads + h] = rin[h]

        query = acc[2, :, columns_of(h)].astype(BF16)
        lifted = query.astype(F32) * jnp.exp(runs[h])
        both_parts = ret[:, columns_of(h)] + jnp.dot(
            lifted, rout[heads + h], preferred_element_type=F32, precision=lax.Precision.HIGHEST
        )
        centred = both_parts - jnp.mean(both_parts, axis=1, keepdims=True)
        spread = jnp.mean(centred * centred, axis=1, keepdims=True)
        ret[:, columns_of(h)] = centred * lax.rsqrt(spread + 1e-05)

    project(4, zs - 1)

    def g_copy(p):
        at = peer(p)
        piece = gated.at[pl.ds(pl.multiple_of(at * frames_here, frames_here), frames_here), :]
        return remote(piece, owned.at[hd], g_send.at[p], g_recv.at[hd], (tm, at))

    def gate_rows(at):
        part = pl.ds(pl.multiple_of(at * frames_here, frames_here), frames_here)
        gate = acc[3, part, :]
        return (gate / (1.0 + jnp.exp(-gate)) * ret[part, :]).astype(BF16)

    for p in range(1, heads_axis):
        at = peer(p)
        part = pl.ds(pl.multiple_of(at * frames_here, frames_here), frames_here)
        gated[part, :] = gate_rows(at)
        g_copy(p).start()
    owned[hd] = gate_rows(hd)

    plane_pass_on(zs - 1)

    def all_out(zo, _):
        for at in range(heads_axis):
            out_landed(at, 2 * zo + 1 - c)
        return 0

    lax.fori_loop(0, zs, all_out, 0)
    for p in range(1, heads_axis):
        at = peer(p)
        remote(owned.at[at], owned.at[at], g_send.at[p], g_recv.at[at], sibling).wait_recv()

    wide = wo_ref.shape[1]

    def finish(t, _):
        total = jnp.zeros((frames_here, wide), F32)
        for at in range(heads_axis):
            total += jnp.dot(owned[at], wo[at, t], preferred_element_type=F32)
        out_ref[:, pl.ds(pl.multiple_of(t * wide, wide), wide)] = total.astype(BF16)
        return 0

    lax.fori_loop(0, tms, finish, 0)

    for p in range(1, heads_axis):
        x_copy(p).wait_send()
        g_copy(p).wait_send()

    @pl.when(c == 0)
    def _():
        for h in range(heads):
            first_copy(h).wait_send()

    @pl.when(c == 1)
    def _():
        for h in range(heads):

            @pl.when(z < zs - 1)
            def _():
                next_copy(h).wait_send()

            @pl.when(z > 0)
            def _():
                share_copy(h).wait_send()

    def drain(zo, _):
        for m in range(5):
            across(m, zo).wait_send()

            @pl.when(jnp.logical_and(zo <= z, z < zs - 1))
            def _():
                along(m, zo, 0).wait_send()

            @pl.when(jnp.logical_and(zo >= z, z > 0))
            def _():
                along(m, zo, 1).wait_send()

        for p in range(1, heads_axis):
            plane(zo, p).wait_send()
            plane_across(zo, p).wait_send()
        return 0

    lax.fori_loop(0, zs, drain, 0)


def solution(mesh):
    tms, heads_axis = mesh.shape["tm"], mesh.shape["head"]
    zs = tms // 2

    def shards(frames, log_decay, w_query, w_key, w_value, w_gate, w_out):
        here, model = frames.shape
        rows, width = w_query.shape
        length, heads = log_decay.shape
        vmem = pl.BlockSpec(memory_space=pltpu.VMEM)
        hbm = pl.BlockSpec(memory_space=pltpu.HBM)
        dma = pltpu.SemaphoreType.DMA
        return pl.pallas_call(
            functools.partial(kernel, tms, heads_axis),
            out_shape=jax.ShapeDtypeStruct((here, model), BF16),
            in_specs=[hbm, vmem] + [hbm] * 5,
            out_specs=vmem,
            scratch_shapes=[
                dma((6,)),
                pltpu.VMEM((length, model), BF16),
                pltpu.VMEM((4, tms, rows, width), BF16),
                pltpu.VMEM((heads_axis, tms) + w_out.shape, BF16),
                pltpu.VMEM((4, length, width), F32),
                pltpu.VMEM((heads, length, length), F32),
                pltpu.VMEM((heads, length, HEAD_DIM), F32),
                pltpu.VMEM((heads, HEAD_DIM + 8, HEAD_DIM), F32),
                pltpu.VMEM((heads, HEAD_DIM + 8, HEAD_DIM), F32),
                pltpu.VMEM((heads, HEAD_DIM, HEAD_DIM), F32),
                pltpu.VMEM((2 * heads, HEAD_DIM, HEAD_DIM), F32),
                pltpu.VMEM((length, width), F32),
                pltpu.VMEM((length, width), BF16),
                pltpu.VMEM((heads_axis, here, width), BF16),
                dma((heads_axis,)),
                dma((heads_axis,)),
                dma((5, zs, 3)),
                dma((4, tms)),
                dma((heads_axis, tms)),
                dma((zs, heads_axis)),
                dma((zs, heads_axis)),
                dma((heads,)),
                dma((heads,)),
                dma((heads,)),
                dma((heads,)),
                dma((heads,)),
                dma((heads_axis,)),
                dma((heads_axis,)),
            ],
            compiler_params=pltpu.CompilerParams(
                collective_id=0, has_side_effects=True, vmem_limit_bytes=50 * 2**20
            ),
        )(frames, log_decay, w_key, w_value, w_query, w_gate, w_out)

    return jax.shard_map(
        shards,
        mesh=mesh,
        in_specs=(
            P(("tm", "head"), None),
            P("tm", "head"),
            P("tm", "head"),
            P("tm", "head"),
            P("tm", "head"),
            P("tm", "head"),
            P("head", "tm"),
        ),
        out_specs=P(("tm", "head"), None),
        check_vma=False,
    )
```

```python
import functools

import jax
import jax.numpy as jnp
from jax import lax
from jax.experimental import pallas as pl
from jax.experimental.pallas import tpu as pltpu
from jax.sharding import PartitionSpec as P

HEAD_DIM = 128
MESH = pl.DeviceIdType.MESH
F32 = jnp.float32
BF16 = jnp.bfloat16


def kernel(
    tms, heads_axis, x_ref, ld_ref, wk_ref, wv_ref, wq_ref, wg_ref, wo_ref, out_ref,
    total, in_sem, x, w, wo, acc, decay, runs, sown, sprev, rin, rout, ret, gated, owned,
    x_send, x_recv, w_send, w_recv, o_recv, oxy_send, osib_send,
    s_send, s_recv, r_send, r_recv, rs_send, g_send, g_recv,
):
    zs = tms // 2
    tm, hd = lax.axis_index("tm"), lax.axis_index("head")
    z, c = lax.div(tm, 2), lax.rem(tm, 2)
    sibling = (2 * z + 1 - c, hd)
    rows = wk_ref.shape[0]
    width = wk_ref.shape[1]
    frames_here = x_ref.shape[0]
    length = frames_here * heads_axis
    heads = width // HEAD_DIM

    def peer(p):
        return lax.rem(hd + p, heads_axis)

    def remote(ref_from, ref_to, send, recv, device):
        return pltpu.make_async_remote_copy(
            src_ref=ref_from, dst_ref=ref_to, send_sem=send, recv_sem=recv,
            device_id=device, device_id_type=MESH,
        )

    def slot(m, position):
        if m == 0:
            return wo.at[hd, position], o_recv.at[hd, position]
        return w.at[m - 1, position], w_recv.at[m - 1, position]

    def along(m, zo, side):
        ref, recv = slot(m, 2 * zo + c)
        to = z + 1 - 2 * side
        return remote(ref, ref, w_send.at[m, zo, side], recv, (2 * to + c, hd))

    def across(m, zo):
        ref, recv = slot(m, 2 * zo + c)
        return remote(ref, ref, w_send.at[m, zo, 2], recv, sibling)

    def landed(m, position):
        ref, recv = slot(m, position)
        remote(ref, ref, w_send.at[m, 0, 2], recv, sibling).wait_recv()

    def plane(zo, p):
        ref = wo.at[hd, 2 * zo + c]
        return remote(ref, ref, oxy_send.at[zo, p], o_recv.at[hd, 2 * zo + c], (tm, peer(p)))

    def plane_across(zo, p):
        at = peer(p)
        ref = wo.at[at, 2 * zo + c]
        return remote(ref, ref, osib_send.at[zo, p], o_recv.at[at, 2 * zo + c], sibling)

    def out_landed(at, position):
        ref = wo.at[at, position]
        remote(ref, ref, osib_send.at[0, 0], o_recv.at[at, position], sibling).wait_recv()

    def both(d, body):
        def one(side, _):
            zo = z - d + 2 * d * side
            first = jnp.logical_or(side == 0, d > 0)

            @pl.when(jnp.logical_and(first, jnp.logical_and(zo >= 0, zo < zs)))
            def _():
                body(zo, side)

            return 0

        lax.fori_loop(0, 2, one, 0)

    def pass_on(m, d):
        def body(zo, side):
            landed(m, 2 * zo + c)
            to = z + 1 - 2 * side

            @pl.when(jnp.logical_and(to >= 0, to < zs))
            def _():
                if m >= 2:
                    along(m - 2, zo, side).wait_send()
                along(m, zo, side).start()

            across(m, zo).start()
            if m == 0:
                for p in range(1, heads_axis):
                    plane(zo, p).start()

        both(d, body)

    def project(m, d):
        def body(zo, side):
            landed(m, 2 * zo + 1 - c)
            columns = pl.ds(pl.multiple_of(zo * (2 * rows), 2 * rows), 2 * rows)
            block = w[m - 1, pl.ds(2 * zo, 2)].reshape(2 * rows, width)
            acc[m - 1] += jnp.dot(x[:, columns], block, preferred_element_type=F32)

        both(d, body)

    def plane_pass_on(d):
        def body(zo, side):
            for p in range(1, heads_axis):
                out_landed(peer(p), 2 * zo + c)
                plane_across(zo, p).start()

        both(d, body)

    barrier = pltpu.get_barrier_semaphore()
    pl.semaphore_signal(barrier, inc=1, device_id=sibling, device_id_type=MESH)
    for p in range(1, heads_axis):
        pl.semaphore_signal(barrier, inc=1, device_id=(tm, peer(p)), device_id_type=MESH)

    @pl.when(z > 0)
    def _():
        pl.semaphore_signal(barrier, inc=1, device_id=(tm - 2, hd), device_id_type=MESH)

    @pl.when(z < zs - 1)
    def _():
        pl.semaphore_signal(barrier, inc=1, device_id=(tm + 2, hd), device_id_type=MESH)

    here = pl.ds(pl.multiple_of(hd * frames_here, frames_here), frames_here)
    own = [
        pltpu.make_async_copy(wo_ref, wo.at[hd, tm], in_sem.at[0]),
        pltpu.make_async_copy(wk_ref, w.at[0, tm], in_sem.at[1]),
        pltpu.make_async_copy(wv_ref, w.at[1, tm], in_sem.at[2]),
        pltpu.make_async_copy(wq_ref, w.at[2, tm], in_sem.at[3]),
        pltpu.make_async_copy(wg_ref, w.at[3, tm], in_sem.at[4]),
        pltpu.make_async_copy(x_ref, x.at[here, :], in_sem.at[5]),
    ]
    for copy in own:
        copy.start()
    neighbours = (z > 0).astype(jnp.int32) + (z < zs - 1).astype(jnp.int32)
    pl.semaphore_wait(barrier, heads_axis + neighbours)

    def x_copy(p):
        return remote(x.at[here, :], x.at[here, :], x_send.at[p], x_recv.at[hd], (tm, peer(p)))

    for m in range(5):
        own[m].wait()

        @pl.when(z < zs - 1)
        def _():
            along(m, z, 0).start()

        @pl.when(z > 0)
        def _():
            along(m, z, 1).start()

        across(m, z).start()
        if m == 0:
            own[5].wait()
            for p in range(1, heads_axis):
                x_copy(p).start()
            for p in range(1, heads_axis):
                plane(z, p).start()

    acc[...] = jnp.zeros_like(acc)
    at_row = lax.broadcasted_iota(jnp.int32, (length, length), 0)
    at_col = lax.broadcasted_iota(jnp.int32, (length, length), 1)
    for h in range(heads):
        steps = ld_ref[h : h + 1, :]
        run_col = jnp.sum(jnp.where(at_row >= at_col, steps, 0.0), axis=1, keepdims=True)
        run_row = jnp.sum(jnp.where(at_row == at_col, run_col, 0.0), axis=0, keepdims=True)
        runs[h] = jnp.broadcast_to(run_col, (length, HEAD_DIM))
        decay[h] = jnp.exp(jnp.where(at_row >= at_col, run_col - run_row, -jnp.inf))
    def frames_landed():
        for p in range(1, heads_axis):
            at = peer(p)
            ref = x.at[pl.ds(pl.multiple_of(at * frames_here, frames_here), frames_here), :]
            remote(ref, ref, x_send.at[p], x_recv.at[at], sibling).wait_recv()

    def lap(d, _):
        for m in range(5):
            pass_on(m, d)

        @pl.when(d == 1)
        def _():
            frames_landed()

        for m in range(1, 5):
            project(m, d - 1)

        @pl.when(d > 1)
        def _():
            plane_pass_on(d - 2)

        return 0

    lax.fori_loop(1, zs - 1, lap, 0)
    for m in range(3):
        pass_on(m, zs - 1)
        if m > 0:
            project(m, zs - 2)
            project(m, zs - 1)

    def columns_of(h):
        return slice(h * HEAD_DIM, (h + 1) * HEAD_DIM)

    def first_copy(h):
        return remote(sown.at[h], sprev.at[h], s_send.at[h], s_recv.at[h], sibling)

    def next_copy(h):
        return remote(rout.at[h], rin.at[h], r_send.at[h], r_recv.at[h], (tm + 2, hd))

    def share_copy(h):
        return remote(rin.at[h], rin.at[h], rs_send.at[h], r_recv.at[h], sibling)

    def state_step(h):
        prior = jnp.exp(sprev[h, HEAD_DIM : HEAD_DIM + 1, :]) * rin[h] + sprev[h, :HEAD_DIM, :]
        rout[h] = jnp.exp(sown[h, HEAD_DIM : HEAD_DIM + 1, :]) * prior + sown[h, :HEAD_DIM, :]
        return prior

    @pl.when(z == 0)
    def _():
        rin[...] = jnp.zeros_like(rin)

    for h in range(heads):
        run = runs[h]
        last = run[length - 1 :, :]
        key = acc[0, :, columns_of(h)].astype(BF16)
        value = acc[1, :, columns_of(h)].astype(BF16)
        scaled = (key.astype(F32) * jnp.exp(last - run)).astype(BF16)
        sown[h, :HEAD_DIM, :] = lax.dot_general(
            scaled, value, (((0,), (0,)), ((), ())), preferred_element_type=F32
        )
        sown[h, HEAD_DIM:, :] = jnp.broadcast_to(last, (8, HEAD_DIM))

        @pl.when(c == 0)
        def _():
            first_copy(h).start()

    @pl.when(jnp.logical_and(c == 1, z == 0))
    def _():
        for h in range(heads):
            first_copy(h).wait_recv()
            state_step(h)
            next_copy(h).start()

    pass_on(3, zs - 1)
    project(3, zs - 2)
    project(3, zs - 1)
    for h in range(heads):
        query = acc[2, :, columns_of(h)].astype(BF16)
        key = acc[0, :, columns_of(h)].astype(BF16)
        value = acc[1, :, columns_of(h)].astype(BF16)
        scores = lax.dot_general(query, key, (((1,), (1,)), ((), ())), preferred_element_type=F32)
        weights = (scores * decay[h]).astype(BF16)
        ret[:, columns_of(h)] = jnp.dot(weights, value, preferred_element_type=F32)
    pass_on(4, zs - 1)
    plane_pass_on(zs - 3)
    plane_pass_on(zs - 2)
    project(4, zs - 2)

    @pl.when(jnp.logical_and(c == 1, z > 0))
    def _():
        for h in range(heads):
            first_copy(h).wait_recv()
        for h in range(heads):
            next_copy(h).wait_recv()
            state_step(h)

            @pl.when(z < zs - 1)
            def _():
                next_copy(h).start()

            share_copy(h).start()

    @pl.when(jnp.logical_and(c == 0, z > 0))
    def _():
        for h in range(heads):
            share_copy(h).wait_recv()

    for h in range(heads):

        @pl.when(c == 1)
        def _():
            rout[heads + h] = (
                jnp.exp(sprev[h, HEAD_DIM : HEAD_DIM + 1, :]) * rin[h] + sprev[h, :HEAD_DIM, :]
            )

        @pl.when(c == 0)
        def _():
            rout[heads + h] = rin[h]

        query = acc[2, :, columns_of(h)].astype(BF16)
        lifted = query.astype(F32) * jnp.exp(runs[h])
        both_parts = ret[:, columns_of(h)] + jnp.dot(
            lifted, rout[heads + h], preferred_element_type=F32, precision=lax.Precision.HIGHEST
        )
        centred = both_parts - jnp.mean(both_parts, axis=1, keepdims=True)
        spread = jnp.mean(centred * centred, axis=1, keepdims=True)
        ret[:, columns_of(h)] = centred * lax.rsqrt(spread + 1e-05)

    project(4, zs - 1)

    def g_copy(p):
        at = peer(p)
        piece = gated.at[pl.ds(pl.multiple_of(at * frames_here, frames_here), frames_here), :]
        return remote(piece, owned.at[hd], g_send.at[p], g_recv.at[hd], (tm, at))

    def gate_rows(at):
        part = pl.ds(pl.multiple_of(at * frames_here, frames_here), frames_here)
        gate = acc[3, part, :]
        return (gate / (1.0 + jnp.exp(-gate)) * ret[part, :]).astype(BF16)

    for p in range(1, heads_axis):
        at = peer(p)
        part = pl.ds(pl.multiple_of(at * frames_here, frames_here), frames_here)
        gated[part, :] = gate_rows(at)
        g_copy(p).start()
    owned[hd] = gate_rows(hd)

    plane_pass_on(zs - 1)

    def all_out(zo, _):
        for at in range(heads_axis):
            out_landed(at, 2 * zo + 1 - c)
        return 0

    lax.fori_loop(0, zs, all_out, 0)
    wide = wo_ref.shape[1]
    for p in range(heads_axis):
        at = peer(p)
        if p > 0:
            remote(owned.at[at], owned.at[at], g_send.at[p], g_recv.at[at], sibling).wait_recv()

        def finish(t, _):
            here = pl.ds(pl.multiple_of(t * wide, wide), wide)
            part = jnp.dot(owned[at], wo[at, t], preferred_element_type=F32)
            if p > 0:
                part += total[:, here]
            if p < heads_axis - 1:
                total[:, here] = part
            else:
                out_ref[:, here] = part.astype(BF16)
            return 0

        lax.fori_loop(0, tms, finish, 0)

    for p in range(1, heads_axis):
        x_copy(p).wait_send()
        g_copy(p).wait_send()

    @pl.when(c == 0)
    def _():
        for h in range(heads):
            first_copy(h).wait_send()

    @pl.when(c == 1)
    def _():
        for h in range(heads):

            @pl.when(z < zs - 1)
            def _():
                next_copy(h).wait_send()

            @pl.when(z > 0)
            def _():
                share_copy(h).wait_send()

    def drain(zo, _):
        for m in range(5):
            across(m, zo).wait_send()

            right, left = (zo <= z, zo >= z) if m >= 3 else (zo == z, zo == z)

            @pl.when(jnp.logical_and(right, z < zs - 1))
            def _():
                along(m, zo, 0).wait_send()

            @pl.when(jnp.logical_and(left, z > 0))
            def _():
                along(m, zo, 1).wait_send()

        for p in range(1, heads_axis):
            plane(zo, p).wait_send()
            plane_across(zo, p).wait_send()
        return 0

    lax.fori_loop(0, zs, drain, 0)


def solution(mesh):
    tms, heads_axis = mesh.shape["tm"], mesh.shape["head"]
    zs = tms // 2

    def shards(frames, log_decay, w_query, w_key, w_value, w_gate, w_out):
        here, model = frames.shape
        rows, width = w_query.shape
        length, heads = log_decay.shape
        vmem = pl.BlockSpec(memory_space=pltpu.VMEM)
        hbm = pl.BlockSpec(memory_space=pltpu.HBM)
        dma = pltpu.SemaphoreType.DMA
        return pl.pallas_call(
            functools.partial(kernel, tms, heads_axis),
            out_shape=jax.ShapeDtypeStruct((here, model), BF16),
            in_specs=[hbm, vmem] + [hbm] * 5,
            out_specs=vmem,
            scratch_shapes=[
                pltpu.VMEM((here, model), F32),
                dma((6,)),
                pltpu.VMEM((length, model), BF16),
                pltpu.VMEM((4, tms, rows, width), BF16),
                pltpu.VMEM((heads_axis, tms) + w_out.shape, BF16),
                pltpu.VMEM((4, length, width), F32),
                pltpu.VMEM((heads, length, length), F32),
                pltpu.VMEM((heads, length, HEAD_DIM), F32),
                pltpu.VMEM((heads, HEAD_DIM + 8, HEAD_DIM), F32),
                pltpu.VMEM((heads, HEAD_DIM + 8, HEAD_DIM), F32),
                pltpu.VMEM((heads, HEAD_DIM, HEAD_DIM), F32),
                pltpu.VMEM((2 * heads, HEAD_DIM, HEAD_DIM), F32),
                pltpu.VMEM((length, width), F32),
                pltpu.VMEM((length, width), BF16),
                pltpu.VMEM((heads_axis, here, width), BF16),
                dma((heads_axis,)),
                dma((heads_axis,)),
                dma((5, zs, 3)),
                dma((4, tms)),
                dma((heads_axis, tms)),
                dma((zs, heads_axis)),
                dma((zs, heads_axis)),
                dma((heads,)),
                dma((heads,)),
                dma((heads,)),
                dma((heads,)),
                dma((heads,)),
                dma((heads_axis,)),
                dma((heads_axis,)),
            ],
            compiler_params=pltpu.CompilerParams(
                collective_id=0, has_side_effects=True, vmem_limit_bytes=62 * 2**20
            ),
        )(frames, log_decay.T, w_key, w_value, w_query, w_gate, w_out)

    return jax.shard_map(
        shards,
        mesh=mesh,
        in_specs=(
            P(("tm", "head"), None),
            P("tm", "head"),
            P("tm", "head"),
            P("tm", "head"),
            P("tm", "head"),
            P("tm", "head"),
            P("head", "tm"),
        ),
        out_specs=P(("tm", "head"), None),
        check_vma=False,
    )
```

```python
import functools

import jax
import jax.numpy as jnp
from jax import lax
from jax.experimental import pallas as pl
from jax.experimental.pallas import tpu as pltpu
from jax.sharding import PartitionSpec as P

HEAD_DIM = 128
MESH = pl.DeviceIdType.MESH
F32 = jnp.float32
BF16 = jnp.bfloat16


def kernel(
    tms, heads_axis, x_ref, ld_ref, wk_ref, wv_ref, wq_ref, wg_ref, wo_ref, out_ref,
    total, in_sem, x, w, wo, acc, decay, runs, sown, sprev, rin, rout, ret, gated, owned,
    x_send, x_recv, w_send, w_recv, o_recv, oxy_send, osib_send,
    s_send, s_recv, r_send, r_recv, rs_send, g_send, g_recv,
):
    zs = tms // 2
    tm, hd = lax.axis_index("tm"), lax.axis_index("head")
    z, c = lax.div(tm, 2), lax.rem(tm, 2)
    sibling = (2 * z + 1 - c, hd)
    rows = wk_ref.shape[0]
    width = wk_ref.shape[1]
    frames_here = x_ref.shape[0]
    length = frames_here * heads_axis
    heads = width // HEAD_DIM

    def peer(p):
        return lax.rem(hd + p, heads_axis)

    def remote(ref_from, ref_to, send, recv, device):
        return pltpu.make_async_remote_copy(
            src_ref=ref_from, dst_ref=ref_to, send_sem=send, recv_sem=recv,
            device_id=device, device_id_type=MESH,
        )

    def slot(m, position):
        if m == 0:
            return wo.at[hd, position], o_recv.at[hd, position]
        return w.at[m - 1, position], w_recv.at[m - 1, position]

    def along(m, zo, side):
        ref, recv = slot(m, 2 * zo + c)
        to = z + 1 - 2 * side
        return remote(ref, ref, w_send.at[m, zo, side], recv, (2 * to + c, hd))

    def across(m, zo):
        ref, recv = slot(m, 2 * zo + c)
        return remote(ref, ref, w_send.at[m, zo, 2], recv, sibling)

    def landed(m, position):
        ref, recv = slot(m, position)
        remote(ref, ref, w_send.at[m, 0, 2], recv, sibling).wait_recv()

    def plane(zo, p):
        ref = wo.at[hd, 2 * zo + c]
        return remote(ref, ref, oxy_send.at[zo, p], o_recv.at[hd, 2 * zo + c], (tm, peer(p)))

    def plane_across(zo, p):
        at = peer(p)
        ref = wo.at[at, 2 * zo + c]
        return remote(ref, ref, osib_send.at[zo, p], o_recv.at[at, 2 * zo + c], sibling)

    def out_landed(at, position):
        ref = wo.at[at, position]
        remote(ref, ref, osib_send.at[0, 0], o_recv.at[at, position], sibling).wait_recv()

    def both(d, body):
        def one(side, _):
            zo = z - d + 2 * d * side
            first = jnp.logical_or(side == 0, d > 0)

            @pl.when(jnp.logical_and(first, jnp.logical_and(zo >= 0, zo < zs)))
            def _():
                body(zo, side)

            return 0

        lax.fori_loop(0, 2, one, 0)

    def pass_on(m, d):
        def body(zo, side):
            landed(m, 2 * zo + c)
            to = z + 1 - 2 * side

            @pl.when(jnp.logical_and(to >= 0, to < zs))
            def _():
                along(m, zo, side).start()

            across(m, zo).start()
            if m == 0:
                for p in range(1, heads_axis):
                    plane(zo, p).start()

        both(d, body)

    def project(m, d):
        def body(zo, side):
            landed(m, 2 * zo + 1 - c)
            columns = pl.ds(pl.multiple_of(zo * (2 * rows), 2 * rows), 2 * rows)
            block = w[m - 1, pl.ds(2 * zo, 2)].reshape(2 * rows, width)
            acc[m - 1] += jnp.dot(x[:, columns], block, preferred_element_type=F32)

        both(d, body)

    def plane_pass_on(d):
        def body(zo, side):
            for p in range(1, heads_axis):
                out_landed(peer(p), 2 * zo + c)
                plane_across(zo, p).start()

        both(d, body)

    barrier = pltpu.get_barrier_semaphore()
    pl.semaphore_signal(barrier, inc=1, device_id=sibling, device_id_type=MESH)
    for p in range(1, heads_axis):
        pl.semaphore_signal(barrier, inc=1, device_id=(tm, peer(p)), device_id_type=MESH)

    @pl.when(z > 0)
    def _():
        pl.semaphore_signal(barrier, inc=1, device_id=(tm - 2, hd), device_id_type=MESH)

    @pl.when(z < zs - 1)
    def _():
        pl.semaphore_signal(barrier, inc=1, device_id=(tm + 2, hd), device_id_type=MESH)

    here = pl.ds(pl.multiple_of(hd * frames_here, frames_here), frames_here)
    own = [
        pltpu.make_async_copy(wo_ref, wo.at[hd, tm], in_sem.at[0]),
        pltpu.make_async_copy(wk_ref, w.at[0, tm], in_sem.at[1]),
        pltpu.make_async_copy(wv_ref, w.at[1, tm], in_sem.at[2]),
        pltpu.make_async_copy(wq_ref, w.at[2, tm], in_sem.at[3]),
        pltpu.make_async_copy(wg_ref, w.at[3, tm], in_sem.at[4]),
        pltpu.make_async_copy(x_ref, x.at[here, :], in_sem.at[5]),
    ]
    for copy in own:
        copy.start()
    neighbours = (z > 0).astype(jnp.int32) + (z < zs - 1).astype(jnp.int32)
    pl.semaphore_wait(barrier, heads_axis + neighbours)

    def x_copy(p):
        return remote(x.at[here, :], x.at[here, :], x_send.at[p], x_recv.at[hd], (tm, peer(p)))

    for m in range(5):
        own[m].wait()

        @pl.when(z < zs - 1)
        def _():
            along(m, z, 0).start()

        @pl.when(z > 0)
        def _():
            along(m, z, 1).start()

        across(m, z).start()
        if m == 0:
            own[5].wait()
            for p in range(1, heads_axis):
                x_copy(p).start()
            for p in range(1, heads_axis):
                plane(z, p).start()

    acc[...] = jnp.zeros_like(acc)
    at_row = lax.broadcasted_iota(jnp.int32, (length, length), 0)
    at_col = lax.broadcasted_iota(jnp.int32, (length, length), 1)
    for h in range(heads):
        steps = ld_ref[h : h + 1, :]
        run_col = jnp.sum(jnp.where(at_row >= at_col, steps, 0.0), axis=1, keepdims=True)
        run_row = jnp.sum(jnp.where(at_row == at_col, run_col, 0.0), axis=0, keepdims=True)
        runs[h] = jnp.broadcast_to(run_col, (length, HEAD_DIM))
        decay[h] = jnp.exp(jnp.where(at_row >= at_col, run_col - run_row, -jnp.inf))
    def frames_landed():
        for p in range(1, heads_axis):
            at = peer(p)
            ref = x.at[pl.ds(pl.multiple_of(at * frames_here, frames_here), frames_here), :]
            remote(ref, ref, x_send.at[p], x_recv.at[at], sibling).wait_recv()

    def lap(d, _):
        for m in range(5):
            pass_on(m, d)

        @pl.when(d == 1)
        def _():
            frames_landed()

        for m in range(1, 5):
            project(m, d - 1)

        @pl.when(d > 1)
        def _():
            plane_pass_on(d - 2)

        return 0

    lax.fori_loop(1, zs - 1, lap, 0)
    for m in range(3):
        pass_on(m, zs - 1)
        if m > 0:
            project(m, zs - 2)
            project(m, zs - 1)

    def columns_of(h):
        return slice(h * HEAD_DIM, (h + 1) * HEAD_DIM)

    def first_copy(h):
        return remote(sown.at[h], sprev.at[h], s_send.at[h], s_recv.at[h], sibling)

    def next_copy(h):
        return remote(rout.at[h], rin.at[h], r_send.at[h], r_recv.at[h], (tm + 2, hd))

    def share_copy(h):
        return remote(rin.at[h], rin.at[h], rs_send.at[h], r_recv.at[h], sibling)

    def state_step(h):
        prior = jnp.exp(sprev[h, HEAD_DIM : HEAD_DIM + 1, :]) * rin[h] + sprev[h, :HEAD_DIM, :]
        rout[h] = jnp.exp(sown[h, HEAD_DIM : HEAD_DIM + 1, :]) * prior + sown[h, :HEAD_DIM, :]
        return prior

    @pl.when(z == 0)
    def _():
        rin[...] = jnp.zeros_like(rin)

    for h in range(heads):
        run = runs[h]
        last = run[length - 1 :, :]
        key = acc[0, :, columns_of(h)].astype(BF16)
        value = acc[1, :, columns_of(h)].astype(BF16)
        scaled = (key.astype(F32) * jnp.exp(last - run)).astype(BF16)
        sown[h, :HEAD_DIM, :] = lax.dot_general(
            scaled, value, (((0,), (0,)), ((), ())), preferred_element_type=F32
        )
        sown[h, HEAD_DIM:, :] = jnp.broadcast_to(last, (8, HEAD_DIM))

        @pl.when(c == 0)
        def _():
            first_copy(h).start()

    @pl.when(jnp.logical_and(c == 1, z == 0))
    def _():
        for h in range(heads):
            first_copy(h).wait_recv()
            state_step(h)
            next_copy(h).start()

    pass_on(3, zs - 1)
    project(3, zs - 2)
    project(3, zs - 1)
    for h in range(heads):
        query = acc[2, :, columns_of(h)].astype(BF16)
        key = acc[0, :, columns_of(h)].astype(BF16)
        value = acc[1, :, columns_of(h)].astype(BF16)
        scores = lax.dot_general(query, key, (((1,), (1,)), ((), ())), preferred_element_type=F32)
        weights = (scores * decay[h]).astype(BF16)
        ret[:, columns_of(h)] = jnp.dot(weights, value, preferred_element_type=F32)
    pass_on(4, zs - 1)
    plane_pass_on(zs - 3)
    plane_pass_on(zs - 2)
    project(4, zs - 2)

    @pl.when(jnp.logical_and(c == 1, z > 0))
    def _():
        for h in range(heads):
            first_copy(h).wait_recv()
        for h in range(heads):
            next_copy(h).wait_recv()
            state_step(h)

            @pl.when(z < zs - 1)
            def _():
                next_copy(h).start()

            share_copy(h).start()

    @pl.when(jnp.logical_and(c == 0, z > 0))
    def _():
        for h in range(heads):
            share_copy(h).wait_recv()

    for h in range(heads):

        @pl.when(c == 1)
        def _():
            rout[heads + h] = (
                jnp.exp(sprev[h, HEAD_DIM : HEAD_DIM + 1, :]) * rin[h] + sprev[h, :HEAD_DIM, :]
            )

        @pl.when(c == 0)
        def _():
            rout[heads + h] = rin[h]

        query = acc[2, :, columns_of(h)].astype(BF16)
        lifted = query.astype(F32) * jnp.exp(runs[h])
        both_parts = ret[:, columns_of(h)] + jnp.dot(
            lifted, rout[heads + h], preferred_element_type=F32, precision=lax.Precision.HIGHEST
        )
        centred = both_parts - jnp.mean(both_parts, axis=1, keepdims=True)
        spread = jnp.mean(centred * centred, axis=1, keepdims=True)
        ret[:, columns_of(h)] = centred * lax.rsqrt(spread + 1e-05)

    plane_pass_on(zs - 1)
    project(4, zs - 1)

    def g_copy(p):
        at = peer(p)
        piece = gated.at[pl.ds(pl.multiple_of(at * frames_here, frames_here), frames_here), :]
        return remote(piece, owned.at[hd], g_send.at[p], g_recv.at[hd], (tm, at))

    def gate_rows(at):
        part = pl.ds(pl.multiple_of(at * frames_here, frames_here), frames_here)
        gate = acc[3, part, :]
        return (gate / (1.0 + jnp.exp(-gate)) * ret[part, :]).astype(BF16)

    for p in range(1, heads_axis):
        at = peer(p)
        part = pl.ds(pl.multiple_of(at * frames_here, frames_here), frames_here)
        gated[part, :] = gate_rows(at)
        g_copy(p).start()
    owned[hd] = gate_rows(hd)

    def all_out(zo, _):
        for at in range(heads_axis):
            out_landed(at, 2 * zo + 1 - c)
        return 0

    lax.fori_loop(0, zs, all_out, 0)
    wide = wo_ref.shape[1]
    for p in range(heads_axis):
        at = peer(p)
        if p > 0:
            remote(owned.at[at], owned.at[at], g_send.at[p], g_recv.at[at], sibling).wait_recv()

        def finish(t, _):
            here = pl.ds(pl.multiple_of(t * wide, wide), wide)
            part = jnp.dot(owned[at], wo[at, t], preferred_element_type=F32)
            if p > 0:
                part += total[:, here]
            if p < heads_axis - 1:
                total[:, here] = part
            else:
                out_ref[:, here] = part.astype(BF16)
            return 0

        lax.fori_loop(0, tms, finish, 0)

    for p in range(1, heads_axis):
        x_copy(p).wait_send()
        g_copy(p).wait_send()

    @pl.when(c == 0)
    def _():
        for h in range(heads):
            first_copy(h).wait_send()

    @pl.when(c == 1)
    def _():
        for h in range(heads):

            @pl.when(z < zs - 1)
            def _():
                next_copy(h).wait_send()

            @pl.when(z > 0)
            def _():
                share_copy(h).wait_send()

    def drain(zo, _):
        for m in range(5):
            across(m, zo).wait_send()

            @pl.when(jnp.logical_and(zo <= z, z < zs - 1))
            def _():
                along(m, zo, 0).wait_send()

            @pl.when(jnp.logical_and(zo >= z, z > 0))
            def _():
                along(m, zo, 1).wait_send()

        for p in range(1, heads_axis):
            plane(zo, p).wait_send()
            plane_across(zo, p).wait_send()
        return 0

    lax.fori_loop(0, zs, drain, 0)


def solution(mesh):
    tms, heads_axis = mesh.shape["tm"], mesh.shape["head"]
    zs = tms // 2

    def shards(frames, log_decay, w_query, w_key, w_value, w_gate, w_out):
        here, model = frames.shape
        rows, width = w_query.shape
        length, heads = log_decay.shape
        vmem = pl.BlockSpec(memory_space=pltpu.VMEM)
        hbm = pl.BlockSpec(memory_space=pltpu.HBM)
        dma = pltpu.SemaphoreType.DMA
        return pl.pallas_call(
            functools.partial(kernel, tms, heads_axis),
            out_shape=jax.ShapeDtypeStruct((here, model), BF16),
            in_specs=[hbm, vmem] + [hbm] * 5,
            out_specs=vmem,
            scratch_shapes=[
                pltpu.VMEM((here, model), F32),
                dma((6,)),
                pltpu.VMEM((length, model), BF16),
                pltpu.VMEM((4, tms, rows, width), BF16),
                pltpu.VMEM((heads_axis, tms) + w_out.shape, BF16),
                pltpu.VMEM((4, length, width), F32),
                pltpu.VMEM((heads, length, length), F32),
                pltpu.VMEM((heads, length, HEAD_DIM), F32),
                pltpu.VMEM((heads, HEAD_DIM + 8, HEAD_DIM), F32),
                pltpu.VMEM((heads, HEAD_DIM + 8, HEAD_DIM), F32),
                pltpu.VMEM((heads, HEAD_DIM, HEAD_DIM), F32),
                pltpu.VMEM((2 * heads, HEAD_DIM, HEAD_DIM), F32),
                pltpu.VMEM((length, width), F32),
                pltpu.VMEM((length, width), BF16),
                pltpu.VMEM((heads_axis, here, width), BF16),
                dma((heads_axis,)),
                dma((heads_axis,)),
                dma((5, zs, 3)),
                dma((4, tms)),
                dma((heads_axis, tms)),
                dma((zs, heads_axis)),
                dma((zs, heads_axis)),
                dma((heads,)),
                dma((heads,)),
                dma((heads,)),
                dma((heads,)),
                dma((heads,)),
                dma((heads_axis,)),
                dma((heads_axis,)),
            ],
            compiler_params=pltpu.CompilerParams(
                collective_id=0, has_side_effects=True, vmem_limit_bytes=62 * 2**20
            ),
        )(frames, log_decay.T, w_key, w_value, w_query, w_gate, w_out)

    return jax.shard_map(
        shards,
        mesh=mesh,
        in_specs=(
            P(("tm", "head"), None),
            P("tm", "head"),
            P("tm", "head"),
            P("tm", "head"),
            P("tm", "head"),
            P("tm", "head"),
            P("head", "tm"),
        ),
        out_specs=P(("tm", "head"), None),
        check_vma=False,
    )
```

```python
import functools

import jax
import jax.numpy as jnp
from jax import lax
from jax.experimental import pallas as pl
from jax.experimental.pallas import tpu as pltpu
from jax.sharding import PartitionSpec as P

HEAD_DIM = 128
MESH = pl.DeviceIdType.MESH
F32 = jnp.float32
BF16 = jnp.bfloat16


def kernel(
    tms, heads_axis, x_ref, ld_ref, wk_ref, wv_ref, wq_ref, wg_ref, wo_ref, out_ref,
    total, in_sem, x, w, wo, acc, decay, runs, sown, sprev, rin, rout, ret, gated, owned,
    x_send, x_recv, w_send, w_recv, o_recv, oxy_send, osib_send,
    s_send, s_recv, r_send, r_recv, rs_send, g_send, g_recv,
):
    zs = tms // 2
    tm, hd = lax.axis_index("tm"), lax.axis_index("head")
    z, c = lax.div(tm, 2), lax.rem(tm, 2)
    sibling = (2 * z + 1 - c, hd)
    rows = wk_ref.shape[0]
    width = wk_ref.shape[1]
    frames_here = x_ref.shape[0]
    length = frames_here * heads_axis
    heads = width // HEAD_DIM

    def peer(p):
        return lax.rem(hd + p, heads_axis)

    def remote(ref_from, ref_to, send, recv, device):
        return pltpu.make_async_remote_copy(
            src_ref=ref_from, dst_ref=ref_to, send_sem=send, recv_sem=recv,
            device_id=device, device_id_type=MESH,
        )

    def slot(m, position):
        if m == 0:
            return wo.at[hd, position], o_recv.at[hd, position]
        return w.at[m - 1, position], w_recv.at[m - 1, position]

    def along(m, zo, side):
        ref, recv = slot(m, 2 * zo + c)
        to = z + 1 - 2 * side
        return remote(ref, ref, w_send.at[m, zo, side], recv, (2 * to + c, hd))

    def across(m, zo):
        ref, recv = slot(m, 2 * zo + c)
        return remote(ref, ref, w_send.at[m, zo, 2], recv, sibling)

    def landed(m, position):
        ref, recv = slot(m, position)
        remote(ref, ref, w_send.at[m, 0, 2], recv, sibling).wait_recv()

    def plane(zo, p):
        ref = wo.at[hd, 2 * zo + c]
        return remote(ref, ref, oxy_send.at[zo, p], o_recv.at[hd, 2 * zo + c], (tm, peer(p)))

    def plane_across(zo, p):
        at = peer(p)
        ref = wo.at[at, 2 * zo + c]
        return remote(ref, ref, osib_send.at[zo, p], o_recv.at[at, 2 * zo + c], sibling)

    def out_landed(at, position):
        ref = wo.at[at, position]
        remote(ref, ref, osib_send.at[0, 0], o_recv.at[at, position], sibling).wait_recv()

    def both(d, body):
        def one(side, _):
            zo = z - d + 2 * d * side
            first = jnp.logical_or(side == 0, d > 0)

            @pl.when(jnp.logical_and(first, jnp.logical_and(zo >= 0, zo < zs)))
            def _():
                body(zo, side)

            return 0

        lax.fori_loop(0, 2, one, 0)

    def pass_on(m, d):
        def body(zo, side):
            landed(m, 2 * zo + c)
            to = z + 1 - 2 * side

            @pl.when(jnp.logical_and(to >= 0, to < zs))
            def _():
                along(m, zo, side).start()

            across(m, zo).start()
            if m == 0:
                for p in range(1, heads_axis):
                    plane(zo, p).start()

        both(d, body)

    def project(m, d):
        def body(zo, side):
            landed(m, 2 * zo + 1 - c)
            columns = pl.ds(pl.multiple_of(zo * (2 * rows), 2 * rows), 2 * rows)
            block = w[m - 1, pl.ds(2 * zo, 2)].reshape(2 * rows, width)
            acc[m - 1] += jnp.dot(x[:, columns], block, preferred_element_type=F32)

        both(d, body)

    def plane_pass_on(d):
        def body(zo, side):
            for p in range(1, heads_axis):
                out_landed(peer(p), 2 * zo + c)
                plane_across(zo, p).start()

        both(d, body)

    barrier = pltpu.get_barrier_semaphore()
    pl.semaphore_signal(barrier, inc=1, device_id=sibling, device_id_type=MESH)
    for p in range(1, heads_axis):
        pl.semaphore_signal(barrier, inc=1, device_id=(tm, peer(p)), device_id_type=MESH)

    @pl.when(z > 0)
    def _():
        pl.semaphore_signal(barrier, inc=1, device_id=(tm - 2, hd), device_id_type=MESH)

    @pl.when(z < zs - 1)
    def _():
        pl.semaphore_signal(barrier, inc=1, device_id=(tm + 2, hd), device_id_type=MESH)

    here = pl.ds(pl.multiple_of(hd * frames_here, frames_here), frames_here)
    own = [
        pltpu.make_async_copy(wo_ref, wo.at[hd, tm], in_sem.at[0]),
        pltpu.make_async_copy(wk_ref, w.at[0, tm], in_sem.at[1]),
        pltpu.make_async_copy(wv_ref, w.at[1, tm], in_sem.at[2]),
        pltpu.make_async_copy(wq_ref, w.at[2, tm], in_sem.at[3]),
        pltpu.make_async_copy(wg_ref, w.at[3, tm], in_sem.at[4]),
        pltpu.make_async_copy(x_ref, x.at[here, :], in_sem.at[5]),
    ]
    for copy in own:
        copy.start()
    neighbours = (z > 0).astype(jnp.int32) + (z < zs - 1).astype(jnp.int32)
    pl.semaphore_wait(barrier, heads_axis + neighbours)

    def x_copy(p):
        return remote(x.at[here, :], x.at[here, :], x_send.at[p], x_recv.at[hd], (tm, peer(p)))

    for m in range(5):
        own[m].wait()

        @pl.when(z < zs - 1)
        def _():
            along(m, z, 0).start()

        @pl.when(z > 0)
        def _():
            along(m, z, 1).start()

        across(m, z).start()
        if m == 0:
            own[5].wait()
            for p in range(1, heads_axis):
                x_copy(p).start()
            for p in range(1, heads_axis):
                plane(z, p).start()

    acc[...] = jnp.zeros_like(acc)
    at_row = lax.broadcasted_iota(jnp.int32, (length, length), 0)
    at_col = lax.broadcasted_iota(jnp.int32, (length, length), 1)
    for h in range(heads):
        steps = ld_ref[h : h + 1, :]
        run_col = jnp.sum(jnp.where(at_row >= at_col, steps, 0.0), axis=1, keepdims=True)
        run_row = jnp.sum(jnp.where(at_row == at_col, run_col, 0.0), axis=0, keepdims=True)
        runs[h] = jnp.broadcast_to(run_col, (length, HEAD_DIM))
        decay[h] = jnp.exp(jnp.where(at_row >= at_col, run_col - run_row, -jnp.inf))
    def frames_landed():
        for p in range(1, heads_axis):
            at = peer(p)
            ref = x.at[pl.ds(pl.multiple_of(at * frames_here, frames_here), frames_here), :]
            remote(ref, ref, x_send.at[p], x_recv.at[at], sibling).wait_recv()

    def lap(d, _):
        for m in range(5):
            pass_on(m, d)
        return 0

    lax.fori_loop(1, zs - 1, lap, 0)
    frames_landed()

    def products(d, _):
        for m in range(1, 5):
            project(m, d)
        plane_pass_on(d)
        return 0

    lax.fori_loop(0, zs - 1, products, 0)
    for m in range(3):
        pass_on(m, zs - 1)
        if m > 0:
            project(m, zs - 1)

    def columns_of(h):
        return slice(h * HEAD_DIM, (h + 1) * HEAD_DIM)

    def first_copy(h):
        return remote(sown.at[h], sprev.at[h], s_send.at[h], s_recv.at[h], sibling)

    def next_copy(h):
        return remote(rout.at[h], rin.at[h], r_send.at[h], r_recv.at[h], (tm + 2, hd))

    def share_copy(h):
        return remote(rin.at[h], rin.at[h], rs_send.at[h], r_recv.at[h], sibling)

    def state_step(h):
        prior = jnp.exp(sprev[h, HEAD_DIM : HEAD_DIM + 1, :]) * rin[h] + sprev[h, :HEAD_DIM, :]
        rout[h] = jnp.exp(sown[h, HEAD_DIM : HEAD_DIM + 1, :]) * prior + sown[h, :HEAD_DIM, :]
        return prior

    @pl.when(z == 0)
    def _():
        rin[...] = jnp.zeros_like(rin)

    for h in range(heads):
        run = runs[h]
        last = run[length - 1 :, :]
        key = acc[0, :, columns_of(h)].astype(BF16)
        value = acc[1, :, columns_of(h)].astype(BF16)
        scaled = (key.astype(F32) * jnp.exp(last - run)).astype(BF16)
        sown[h, :HEAD_DIM, :] = lax.dot_general(
            scaled, value, (((0,), (0,)), ((), ())), preferred_element_type=F32
        )
        sown[h, HEAD_DIM:, :] = jnp.broadcast_to(last, (8, HEAD_DIM))

        @pl.when(c == 0)
        def _():
            first_copy(h).start()

    @pl.when(jnp.logical_and(c == 1, z == 0))
    def _():
        for h in range(heads):
            first_copy(h).wait_recv()
            state_step(h)
            next_copy(h).start()

    pass_on(3, zs - 1)
    project(3, zs - 1)
    for h in range(heads):
        query = acc[2, :, columns_of(h)].astype(BF16)
        key = acc[0, :, columns_of(h)].astype(BF16)
        value = acc[1, :, columns_of(h)].astype(BF16)
        scores = lax.dot_general(query, key, (((1,), (1,)), ((), ())), preferred_element_type=F32)
        weights = (scores * decay[h]).astype(BF16)
        ret[:, columns_of(h)] = jnp.dot(weights, value, preferred_element_type=F32)
    pass_on(4, zs - 1)

    @pl.when(jnp.logical_and(c == 1, z > 0))
    def _():
        for h in range(heads):
            first_copy(h).wait_recv()
        for h in range(heads):
            next_copy(h).wait_recv()
            state_step(h)

            @pl.when(z < zs - 1)
            def _():
                next_copy(h).start()

            share_copy(h).start()

    @pl.when(jnp.logical_and(c == 0, z > 0))
    def _():
        for h in range(heads):
            share_copy(h).wait_recv()

    for h in range(heads):

        @pl.when(c == 1)
        def _():
            rout[heads + h] = (
                jnp.exp(sprev[h, HEAD_DIM : HEAD_DIM + 1, :]) * rin[h] + sprev[h, :HEAD_DIM, :]
            )

        @pl.when(c == 0)
        def _():
            rout[heads + h] = rin[h]

        query = acc[2, :, columns_of(h)].astype(BF16)
        lifted = query.astype(F32) * jnp.exp(runs[h])
        both_parts = ret[:, columns_of(h)] + jnp.dot(
            lifted, rout[heads + h], preferred_element_type=F32, precision=lax.Precision.HIGHEST
        )
        centred = both_parts - jnp.mean(both_parts, axis=1, keepdims=True)
        spread = jnp.mean(centred * centred, axis=1, keepdims=True)
        ret[:, columns_of(h)] = centred * lax.rsqrt(spread + 1e-05)

    plane_pass_on(zs - 1)
    project(4, zs - 1)

    def g_copy(p):
        at = peer(p)
        piece = gated.at[pl.ds(pl.multiple_of(at * frames_here, frames_here), frames_here), :]
        return remote(piece, owned.at[hd], g_send.at[p], g_recv.at[hd], (tm, at))

    def gate_rows(at):
        part = pl.ds(pl.multiple_of(at * frames_here, frames_here), frames_here)
        gate = acc[3, part, :]
        return (gate / (1.0 + jnp.exp(-gate)) * ret[part, :]).astype(BF16)

    for p in range(1, heads_axis):
        at = peer(p)
        part = pl.ds(pl.multiple_of(at * frames_here, frames_here), frames_here)
        gated[part, :] = gate_rows(at)
        g_copy(p).start()
    owned[hd] = gate_rows(hd)

    def all_out(zo, _):
        for at in range(heads_axis):
            out_landed(at, 2 * zo + 1 - c)
        return 0

    lax.fori_loop(0, zs, all_out, 0)
    wide = wo_ref.shape[1]
    for p in range(heads_axis):
        at = peer(p)
        if p > 0:
            remote(owned.at[at], owned.at[at], g_send.at[p], g_recv.at[at], sibling).wait_recv()

        def finish(t, _):
            here = pl.ds(pl.multiple_of(t * wide, wide), wide)
            part = jnp.dot(owned[at], wo[at, t], preferred_element_type=F32)
            if p > 0:
                part += total[:, here]
            if p < heads_axis - 1:
                total[:, here] = part
            else:
                out_ref[:, here] = part.astype(BF16)
            return 0

        lax.fori_loop(0, tms, finish, 0)

    for p in range(1, heads_axis):
        x_copy(p).wait_send()
        g_copy(p).wait_send()

    @pl.when(c == 0)
    def _():
        for h in range(heads):
            first_copy(h).wait_send()

    @pl.when(c == 1)
    def _():
        for h in range(heads):

            @pl.when(z < zs - 1)
            def _():
                next_copy(h).wait_send()

            @pl.when(z > 0)
            def _():
                share_copy(h).wait_send()

    def drain(zo, _):
        for m in range(5):
            across(m, zo).wait_send()

            @pl.when(jnp.logical_and(zo <= z, z < zs - 1))
            def _():
                along(m, zo, 0).wait_send()

            @pl.when(jnp.logical_and(zo >= z, z > 0))
            def _():
                along(m, zo, 1).wait_send()

        for p in range(1, heads_axis):
            plane(zo, p).wait_send()
            plane_across(zo, p).wait_send()
        return 0

    lax.fori_loop(0, zs, drain, 0)


def solution(mesh):
    tms, heads_axis = mesh.shape["tm"], mesh.shape["head"]
    zs = tms // 2

    def shards(frames, log_decay, w_query, w_key, w_value, w_gate, w_out):
        here, model = frames.shape
        rows, width = w_query.shape
        length, heads = log_decay.shape
        vmem = pl.BlockSpec(memory_space=pltpu.VMEM)
        hbm = pl.BlockSpec(memory_space=pltpu.HBM)
        dma = pltpu.SemaphoreType.DMA
        return pl.pallas_call(
            functools.partial(kernel, tms, heads_axis),
            out_shape=jax.ShapeDtypeStruct((here, model), BF16),
            in_specs=[hbm, vmem] + [hbm] * 5,
            out_specs=vmem,
            scratch_shapes=[
                pltpu.VMEM((here, model), F32),
                dma((6,)),
                pltpu.VMEM((length, model), BF16),
                pltpu.VMEM((4, tms, rows, width), BF16),
                pltpu.VMEM((heads_axis, tms) + w_out.shape, BF16),
                pltpu.VMEM((4, length, width), F32),
                pltpu.VMEM((heads, length, length), F32),
                pltpu.VMEM((heads, length, HEAD_DIM), F32),
                pltpu.VMEM((heads, HEAD_DIM + 8, HEAD_DIM), F32),
                pltpu.VMEM((heads, HEAD_DIM + 8, HEAD_DIM), F32),
                pltpu.VMEM((heads, HEAD_DIM, HEAD_DIM), F32),
                pltpu.VMEM((2 * heads, HEAD_DIM, HEAD_DIM), F32),
                pltpu.VMEM((length, width), F32),
                pltpu.VMEM((length, width), BF16),
                pltpu.VMEM((heads_axis, here, width), BF16),
                dma((heads_axis,)),
                dma((heads_axis,)),
                dma((5, zs, 3)),
                dma((4, tms)),
                dma((heads_axis, tms)),
                dma((zs, heads_axis)),
                dma((zs, heads_axis)),
                dma((heads,)),
                dma((heads,)),
                dma((heads,)),
                dma((heads,)),
                dma((heads,)),
                dma((heads_axis,)),
                dma((heads_axis,)),
            ],
            compiler_params=pltpu.CompilerParams(
                collective_id=0, has_side_effects=True, vmem_limit_bytes=62 * 2**20
            ),
        )(frames, log_decay.T, w_key, w_value, w_query, w_gate, w_out)

    return jax.shard_map(
        shards,
        mesh=mesh,
        in_specs=(
            P(("tm", "head"), None),
            P("tm", "head"),
            P("tm", "head"),
            P("tm", "head"),
            P("tm", "head"),
            P("tm", "head"),
            P("head", "tm"),
        ),
        out_specs=P(("tm", "head"), None),
        check_vma=False,
    )
```

```python
import functools

import jax
import jax.numpy as jnp
from jax import lax
from jax.experimental import pallas as pl
from jax.experimental.pallas import tpu as pltpu
from jax.sharding import PartitionSpec as P

HEAD_DIM = 128
MESH = pl.DeviceIdType.MESH
F32 = jnp.float32
BF16 = jnp.bfloat16


def kernel(
    tms, heads_axis, x_ref, ld_ref, wk_ref, wv_ref, wq_ref, wg_ref, wo_ref, out_ref,
    total, in_sem, x, w, wo, acc, decay, runs, sown, sprev, rin, rout, ret, gated, owned,
    x_send, x_recv, w_send, w_recv, o_recv, oxy_send, osib_send,
    s_send, s_recv, r_send, r_recv, rs_send, g_send, g_recv,
):
    zs = tms // 2
    tm, hd = lax.axis_index("tm"), lax.axis_index("head")
    z, c = lax.div(tm, 2), lax.rem(tm, 2)
    sibling = (2 * z + 1 - c, hd)
    rows = wk_ref.shape[0]
    width = wk_ref.shape[1]
    frames_here = x_ref.shape[0]
    length = frames_here * heads_axis
    heads = width // HEAD_DIM
    parts = 2 if heads % 2 == 0 else 1
    part_width = width // parts
    kinds = 4 + parts

    def gate_columns(part):
        return slice(part * part_width, (part + 1) * part_width)

    def peer(p):
        return lax.rem(hd + p, heads_axis)

    def remote(ref_from, ref_to, send, recv, device):
        return pltpu.make_async_remote_copy(
            src_ref=ref_from, dst_ref=ref_to, send_sem=send, recv_sem=recv,
            device_id=device, device_id_type=MESH,
        )

    def slot(m, position):
        if m == 0:
            return wo.at[hd, position], o_recv.at[hd, position]
        if m >= 4:
            return w.at[3, position, :, gate_columns(m - 4)], w_recv.at[m - 1, position]
        return w.at[m - 1, position], w_recv.at[m - 1, position]

    def along(m, zo, side):
        ref, recv = slot(m, 2 * zo + c)
        to = z + 1 - 2 * side
        return remote(ref, ref, w_send.at[m, zo, side], recv, (2 * to + c, hd))

    def across(m, zo):
        ref, recv = slot(m, 2 * zo + c)
        return remote(ref, ref, w_send.at[m, zo, 2], recv, sibling)

    def landed(m, position):
        ref, recv = slot(m, position)
        remote(ref, ref, w_send.at[m, 0, 2], recv, sibling).wait_recv()

    def plane(zo, p):
        ref = wo.at[hd, 2 * zo + c]
        return remote(ref, ref, oxy_send.at[zo, p], o_recv.at[hd, 2 * zo + c], (tm, peer(p)))

    def plane_across(zo, p):
        at = peer(p)
        ref = wo.at[at, 2 * zo + c]
        return remote(ref, ref, osib_send.at[zo, p], o_recv.at[at, 2 * zo + c], sibling)

    def out_landed(at, position):
        ref = wo.at[at, position]
        remote(ref, ref, osib_send.at[0, 0], o_recv.at[at, position], sibling).wait_recv()

    def both(d, body):
        def one(side, _):
            zo = z - d + 2 * d * side
            first = jnp.logical_or(side == 0, d > 0)

            @pl.when(jnp.logical_and(first, jnp.logical_and(zo >= 0, zo < zs)))
            def _():
                body(zo, side)

            return 0

        lax.fori_loop(0, 2, one, 0)

    def pass_on(m, d):
        def body(zo, side):
            landed(m, 2 * zo + c)
            to = z + 1 - 2 * side

            @pl.when(jnp.logical_and(to >= 0, to < zs))
            def _():
                along(m, zo, side).start()

            across(m, zo).start()
            if m == 0:
                for p in range(1, heads_axis):
                    plane(zo, p).start()

        both(d, body)

    def project(m, d):
        def body(zo, side):
            landed(m, 2 * zo + 1 - c)
            columns = pl.ds(pl.multiple_of(zo * (2 * rows), 2 * rows), 2 * rows)
            out = gate_columns(m - 4) if m >= 4 else slice(0, width)
            at = min(m - 1, 3)
            block = w[at, pl.ds(2 * zo, 2), :, out].reshape(2 * rows, out.stop - out.start)
            acc[at, :, out] += jnp.dot(x[:, columns], block, preferred_element_type=F32)

        both(d, body)

    def plane_pass_on(d):
        def body(zo, side):
            for p in range(1, heads_axis):
                out_landed(peer(p), 2 * zo + c)
                plane_across(zo, p).start()

        both(d, body)

    barrier = pltpu.get_barrier_semaphore()
    pl.semaphore_signal(barrier, inc=1, device_id=sibling, device_id_type=MESH)
    for p in range(1, heads_axis):
        pl.semaphore_signal(barrier, inc=1, device_id=(tm, peer(p)), device_id_type=MESH)

    @pl.when(z > 0)
    def _():
        pl.semaphore_signal(barrier, inc=1, device_id=(tm - 2, hd), device_id_type=MESH)

    @pl.when(z < zs - 1)
    def _():
        pl.semaphore_signal(barrier, inc=1, device_id=(tm + 2, hd), device_id_type=MESH)

    here = pl.ds(pl.multiple_of(hd * frames_here, frames_here), frames_here)
    own = [
        pltpu.make_async_copy(wo_ref, wo.at[hd, tm], in_sem.at[0]),
        pltpu.make_async_copy(wk_ref, w.at[0, tm], in_sem.at[1]),
        pltpu.make_async_copy(wv_ref, w.at[1, tm], in_sem.at[2]),
        pltpu.make_async_copy(wq_ref, w.at[2, tm], in_sem.at[3]),
        pltpu.make_async_copy(wg_ref, w.at[3, tm], in_sem.at[4]),
        pltpu.make_async_copy(x_ref, x.at[here, :], in_sem.at[5]),
    ]
    for copy in own:
        copy.start()
    neighbours = (z > 0).astype(jnp.int32) + (z < zs - 1).astype(jnp.int32)
    pl.semaphore_wait(barrier, heads_axis + neighbours)

    def x_copy(p):
        return remote(x.at[here, :], x.at[here, :], x_send.at[p], x_recv.at[hd], (tm, peer(p)))

    for m in range(kinds):
        if m < 5:
            own[m].wait()

        @pl.when(z < zs - 1)
        def _():
            along(m, z, 0).start()

        @pl.when(z > 0)
        def _():
            along(m, z, 1).start()

        across(m, z).start()
        if m == 0:
            own[5].wait()
            for p in range(1, heads_axis):
                x_copy(p).start()
            for p in range(1, heads_axis):
                plane(z, p).start()

    acc[...] = jnp.zeros_like(acc)
    at_row = lax.broadcasted_iota(jnp.int32, (length, length), 0)
    at_col = lax.broadcasted_iota(jnp.int32, (length, length), 1)
    for h in range(heads):
        steps = ld_ref[h : h + 1, :]
        run_col = jnp.sum(jnp.where(at_row >= at_col, steps, 0.0), axis=1, keepdims=True)
        run_row = jnp.sum(jnp.where(at_row == at_col, run_col, 0.0), axis=0, keepdims=True)
        runs[h] = jnp.broadcast_to(run_col, (length, HEAD_DIM))
        decay[h] = jnp.exp(jnp.where(at_row >= at_col, run_col - run_row, -jnp.inf))
    def frames_landed():
        for p in range(1, heads_axis):
            at = peer(p)
            ref = x.at[pl.ds(pl.multiple_of(at * frames_here, frames_here), frames_here), :]
            remote(ref, ref, x_send.at[p], x_recv.at[at], sibling).wait_recv()

    def lap(d, _):
        for m in range(kinds):
            pass_on(m, d)
        return 0

    lax.fori_loop(1, zs - 1, lap, 0)
    frames_landed()

    def products(d, _):
        for m in range(1, kinds):
            project(m, d)
        plane_pass_on(d)
        return 0

    lax.fori_loop(0, zs - 1, products, 0)
    for m in range(3):
        pass_on(m, zs - 1)
        if m > 0:
            project(m, zs - 1)

    def columns_of(h):
        return slice(h * HEAD_DIM, (h + 1) * HEAD_DIM)

    def first_copy(h):
        return remote(sown.at[h], sprev.at[h], s_send.at[h], s_recv.at[h], sibling)

    def next_copy(h):
        return remote(rout.at[h], rin.at[h], r_send.at[h], r_recv.at[h], (tm + 2, hd))

    def share_copy(h):
        return remote(rin.at[h], rin.at[h], rs_send.at[h], r_recv.at[h], sibling)

    def state_step(h):
        prior = jnp.exp(sprev[h, HEAD_DIM : HEAD_DIM + 1, :]) * rin[h] + sprev[h, :HEAD_DIM, :]
        rout[h] = jnp.exp(sown[h, HEAD_DIM : HEAD_DIM + 1, :]) * prior + sown[h, :HEAD_DIM, :]
        return prior

    @pl.when(z == 0)
    def _():
        rin[...] = jnp.zeros_like(rin)

    for h in range(heads):
        run = runs[h]
        last = run[length - 1 :, :]
        key = acc[0, :, columns_of(h)].astype(BF16)
        value = acc[1, :, columns_of(h)].astype(BF16)
        scaled = (key.astype(F32) * jnp.exp(last - run)).astype(BF16)
        sown[h, :HEAD_DIM, :] = lax.dot_general(
            scaled, value, (((0,), (0,)), ((), ())), preferred_element_type=F32
        )
        sown[h, HEAD_DIM:, :] = jnp.broadcast_to(last, (8, HEAD_DIM))

        @pl.when(c == 0)
        def _():
            first_copy(h).start()

    @pl.when(jnp.logical_and(c == 1, z == 0))
    def _():
        for h in range(heads):
            first_copy(h).wait_recv()
            state_step(h)
            next_copy(h).start()

    pass_on(3, zs - 1)
    project(3, zs - 1)
    for h in range(heads):
        query = acc[2, :, columns_of(h)].astype(BF16)
        key = acc[0, :, columns_of(h)].astype(BF16)
        value = acc[1, :, columns_of(h)].astype(BF16)
        scores = lax.dot_general(query, key, (((1,), (1,)), ((), ())), preferred_element_type=F32)
        weights = (scores * decay[h]).astype(BF16)
        ret[:, columns_of(h)] = jnp.dot(weights, value, preferred_element_type=F32)
    pass_on(4, zs - 1)

    @pl.when(jnp.logical_and(c == 1, z > 0))
    def _():
        for h in range(heads):
            first_copy(h).wait_recv()
        for h in range(heads):
            next_copy(h).wait_recv()
            state_step(h)

            @pl.when(z < zs - 1)
            def _():
                next_copy(h).start()

            share_copy(h).start()

    @pl.when(jnp.logical_and(c == 0, z > 0))
    def _():
        for h in range(heads):
            share_copy(h).wait_recv()

    for h in range(heads):

        @pl.when(c == 1)
        def _():
            rout[heads + h] = (
                jnp.exp(sprev[h, HEAD_DIM : HEAD_DIM + 1, :]) * rin[h] + sprev[h, :HEAD_DIM, :]
            )

        @pl.when(c == 0)
        def _():
            rout[heads + h] = rin[h]

        query = acc[2, :, columns_of(h)].astype(BF16)
        lifted = query.astype(F32) * jnp.exp(runs[h])
        both_parts = ret[:, columns_of(h)] + jnp.dot(
            lifted, rout[heads + h], preferred_element_type=F32, precision=lax.Precision.HIGHEST
        )
        centred = both_parts - jnp.mean(both_parts, axis=1, keepdims=True)
        spread = jnp.mean(centred * centred, axis=1, keepdims=True)
        ret[:, columns_of(h)] = centred * lax.rsqrt(spread + 1e-05)

    plane_pass_on(zs - 1)
    def rows_of(at):
        return pl.ds(pl.multiple_of(at * frames_here, frames_here), frames_here)

    def g_copy(p, part):
        at, out = peer(p), gate_columns(part)
        return remote(
            gated.at[rows_of(at), out], owned.at[hd, :, out],
            g_send.at[p, part], g_recv.at[hd, part], (tm, at),
        )

    def gate_rows(at, part):
        out = gate_columns(part)
        gate = acc[3, rows_of(at), out]
        return (gate / (1.0 + jnp.exp(-gate)) * ret[rows_of(at), out]).astype(BF16)

    for part in range(parts):
        if part > 0:
            pass_on(4 + part, zs - 1)
        project(4 + part, zs - 1)
        for p in range(1, heads_axis):
            gated[rows_of(peer(p)), gate_columns(part)] = gate_rows(peer(p), part)
            g_copy(p, part).start()
        owned[hd, :, gate_columns(part)] = gate_rows(hd, part)

    def all_out(zo, _):
        for at in range(heads_axis):
            out_landed(at, 2 * zo + 1 - c)
        return 0

    lax.fori_loop(0, zs, all_out, 0)
    wide = wo_ref.shape[1]
    for part in range(parts):
        out = gate_columns(part)
        for p in range(1, heads_axis):
            ref = owned.at[peer(p), :, out]
            remote(ref, ref, g_send.at[p, part], g_recv.at[peer(p), part], sibling).wait_recv()

        def finish(t, _):
            here = pl.ds(pl.multiple_of(t * wide, wide), wide)
            piece = jnp.zeros((frames_here, wide), F32) if part == 0 else total[:, here]
            for at in range(heads_axis):
                piece += jnp.dot(owned[at, :, out], wo[at, t, out, :], preferred_element_type=F32)
            if part < parts - 1:
                total[:, here] = piece
            else:
                out_ref[:, here] = piece.astype(BF16)
            return 0

        lax.fori_loop(0, tms, finish, 0)

    for p in range(1, heads_axis):
        x_copy(p).wait_send()
        for part in range(parts):
            g_copy(p, part).wait_send()

    @pl.when(c == 0)
    def _():
        for h in range(heads):
            first_copy(h).wait_send()

    @pl.when(c == 1)
    def _():
        for h in range(heads):

            @pl.when(z < zs - 1)
            def _():
                next_copy(h).wait_send()

            @pl.when(z > 0)
            def _():
                share_copy(h).wait_send()

    def drain(zo, _):
        for m in range(kinds):
            across(m, zo).wait_send()

            @pl.when(jnp.logical_and(zo <= z, z < zs - 1))
            def _():
                along(m, zo, 0).wait_send()

            @pl.when(jnp.logical_and(zo >= z, z > 0))
            def _():
                along(m, zo, 1).wait_send()

        for p in range(1, heads_axis):
            plane(zo, p).wait_send()
            plane_across(zo, p).wait_send()
        return 0

    lax.fori_loop(0, zs, drain, 0)


def solution(mesh):
    tms, heads_axis = mesh.shape["tm"], mesh.shape["head"]
    zs = tms // 2

    def shards(frames, log_decay, w_query, w_key, w_value, w_gate, w_out):
        here, model = frames.shape
        rows, width = w_query.shape
        length, heads = log_decay.shape
        vmem = pl.BlockSpec(memory_space=pltpu.VMEM)
        hbm = pl.BlockSpec(memory_space=pltpu.HBM)
        dma = pltpu.SemaphoreType.DMA
        return pl.pallas_call(
            functools.partial(kernel, tms, heads_axis),
            out_shape=jax.ShapeDtypeStruct((here, model), BF16),
            in_specs=[hbm, vmem] + [hbm] * 5,
            out_specs=vmem,
            scratch_shapes=[
                pltpu.VMEM((here, model), F32),
                dma((6,)),
                pltpu.VMEM((length, model), BF16),
                pltpu.VMEM((4, tms, rows, width), BF16),
                pltpu.VMEM((heads_axis, tms) + w_out.shape, BF16),
                pltpu.VMEM((4, length, width), F32),
                pltpu.VMEM((heads, length, length), F32),
                pltpu.VMEM((heads, length, HEAD_DIM), F32),
                pltpu.VMEM((heads, HEAD_DIM + 8, HEAD_DIM), F32),
                pltpu.VMEM((heads, HEAD_DIM + 8, HEAD_DIM), F32),
                pltpu.VMEM((heads, HEAD_DIM, HEAD_DIM), F32),
                pltpu.VMEM((2 * heads, HEAD_DIM, HEAD_DIM), F32),
                pltpu.VMEM((length, width), F32),
                pltpu.VMEM((length, width), BF16),
                pltpu.VMEM((heads_axis, here, width), BF16),
                dma((heads_axis,)),
                dma((heads_axis,)),
                dma((6, zs, 3)),
                dma((5, tms)),
                dma((heads_axis, tms)),
                dma((zs, heads_axis)),
                dma((zs, heads_axis)),
                dma((heads,)),
                dma((heads,)),
                dma((heads,)),
                dma((heads,)),
                dma((heads,)),
                dma((heads_axis, 2)),
                dma((heads_axis, 2)),
            ],
            compiler_params=pltpu.CompilerParams(
                collective_id=0, has_side_effects=True, vmem_limit_bytes=62 * 2**20
            ),
        )(frames, log_decay.T, w_key, w_value, w_query, w_gate, w_out)

    return jax.shard_map(
        shards,
        mesh=mesh,
        in_specs=(
            P(("tm", "head"), None),
            P("tm", "head"),
            P("tm", "head"),
            P("tm", "head"),
            P("tm", "head"),
            P("tm", "head"),
            P("head", "tm"),
        ),
        out_specs=P(("tm", "head"), None),
        check_vma=False,
    )
```

```python
import functools

import jax
import jax.numpy as jnp
from jax import lax
from jax.experimental import pallas as pl
from jax.experimental.pallas import tpu as pltpu
from jax.sharding import PartitionSpec as P

HEAD_DIM = 128
MESH = pl.DeviceIdType.MESH
F32 = jnp.float32
BF16 = jnp.bfloat16


def kernel(
    tms, heads_axis, x_ref, ld_ref, wk_ref, wv_ref, wq_ref, wg_ref, wo_ref, out_ref,
    total, in_sem, x, w, wo, acc, decay, runs, sown, sprev, rin, rout, ret, gated, owned,
    x_send, x_recv, w_send, w_recv, o_recv, oxy_send, osib_send,
    s_send, s_recv, r_send, r_recv, rs_send, g_send, g_recv,
):
    zs = tms // 2
    tm, hd = lax.axis_index("tm"), lax.axis_index("head")
    z, c = lax.div(tm, 2), lax.rem(tm, 2)
    sibling = (2 * z + 1 - c, hd)
    rows = wk_ref.shape[0]
    width = wk_ref.shape[1]
    frames_here = x_ref.shape[0]
    length = frames_here * heads_axis
    heads = width // HEAD_DIM
    parts = 2 if heads % 2 == 0 else 1
    part_width = width // parts
    kinds = 4 + parts
    order = (1, 2, 0) + tuple(range(3, kinds))

    def gate_columns(part):
        return slice(part * part_width, (part + 1) * part_width)

    def peer(p):
        return lax.rem(hd + p, heads_axis)

    def remote(ref_from, ref_to, send, recv, device):
        return pltpu.make_async_remote_copy(
            src_ref=ref_from, dst_ref=ref_to, send_sem=send, recv_sem=recv,
            device_id=device, device_id_type=MESH,
        )

    def slot(m, position):
        if m == 0:
            return wo.at[hd, position], o_recv.at[hd, position]
        if m >= 4:
            return w.at[3, position, :, gate_columns(m - 4)], w_recv.at[m - 1, position]
        return w.at[m - 1, position], w_recv.at[m - 1, position]

    def along(m, zo, side):
        ref, recv = slot(m, 2 * zo + c)
        to = z + 1 - 2 * side
        return remote(ref, ref, w_send.at[m, zo, side], recv, (2 * to + c, hd))

    def across(m, zo):
        ref, recv = slot(m, 2 * zo + c)
        return remote(ref, ref, w_send.at[m, zo, 2], recv, sibling)

    def landed(m, position):
        ref, recv = slot(m, position)
        remote(ref, ref, w_send.at[m, 0, 2], recv, sibling).wait_recv()

    def plane(zo, p):
        ref = wo.at[hd, 2 * zo + c]
        return remote(ref, ref, oxy_send.at[zo, p], o_recv.at[hd, 2 * zo + c], (tm, peer(p)))

    def plane_across(zo, p):
        at = peer(p)
        ref = wo.at[at, 2 * zo + c]
        return remote(ref, ref, osib_send.at[zo, p], o_recv.at[at, 2 * zo + c], sibling)

    def out_landed(at, position):
        ref = wo.at[at, position]
        remote(ref, ref, osib_send.at[0, 0], o_recv.at[at, position], sibling).wait_recv()

    def both(d, body):
        def one(side, _):
            zo = z - d + 2 * d * side
            first = jnp.logical_or(side == 0, d > 0)

            @pl.when(jnp.logical_and(first, jnp.logical_and(zo >= 0, zo < zs)))
            def _():
                body(zo, side)

            return 0

        lax.fori_loop(0, 2, one, 0)

    def pass_on(m, d):
        def body(zo, side):
            landed(m, 2 * zo + c)
            to = z + 1 - 2 * side

            @pl.when(jnp.logical_and(to >= 0, to < zs))
            def _():
                along(m, zo, side).start()

            across(m, zo).start()
            if m == 0:
                for p in range(1, heads_axis):
                    plane(zo, p).start()

        both(d, body)

    def project(m, d):
        def body(zo, side):
            landed(m, 2 * zo + 1 - c)
            columns = pl.ds(pl.multiple_of(zo * (2 * rows), 2 * rows), 2 * rows)
            out = gate_columns(m - 4) if m >= 4 else slice(0, width)
            at = min(m - 1, 3)
            block = w[at, pl.ds(2 * zo, 2), :, out].reshape(2 * rows, out.stop - out.start)
            acc[at, :, out] += jnp.dot(x[:, columns], block, preferred_element_type=F32)

        both(d, body)

    def plane_pass_on(d):
        def body(zo, side):
            for p in range(1, heads_axis):
                out_landed(peer(p), 2 * zo + c)
                plane_across(zo, p).start()

        both(d, body)

    barrier = pltpu.get_barrier_semaphore()
    pl.semaphore_signal(barrier, inc=1, device_id=sibling, device_id_type=MESH)
    for p in range(1, heads_axis):
        pl.semaphore_signal(barrier, inc=1, device_id=(tm, peer(p)), device_id_type=MESH)

    @pl.when(z > 0)
    def _():
        pl.semaphore_signal(barrier, inc=1, device_id=(tm - 2, hd), device_id_type=MESH)

    @pl.when(z < zs - 1)
    def _():
        pl.semaphore_signal(barrier, inc=1, device_id=(tm + 2, hd), device_id_type=MESH)

    here = pl.ds(pl.multiple_of(hd * frames_here, frames_here), frames_here)
    own = [
        pltpu.make_async_copy(wo_ref, wo.at[hd, tm], in_sem.at[0]),
        pltpu.make_async_copy(wk_ref, w.at[0, tm], in_sem.at[1]),
        pltpu.make_async_copy(wv_ref, w.at[1, tm], in_sem.at[2]),
        pltpu.make_async_copy(wq_ref, w.at[2, tm], in_sem.at[3]),
        pltpu.make_async_copy(wg_ref, w.at[3, tm], in_sem.at[4]),
        pltpu.make_async_copy(x_ref, x.at[here, :], in_sem.at[5]),
    ]
    for copy in own:
        copy.start()
    neighbours = (z > 0).astype(jnp.int32) + (z < zs - 1).astype(jnp.int32)
    pl.semaphore_wait(barrier, heads_axis + neighbours)

    def x_copy(p):
        return remote(x.at[here, :], x.at[here, :], x_send.at[p], x_recv.at[hd], (tm, peer(p)))

    for m in order:
        if m < 5:
            own[m].wait()

        @pl.when(z < zs - 1)
        def _():
            along(m, z, 0).start()

        @pl.when(z > 0)
        def _():
            along(m, z, 1).start()

        across(m, z).start()
        if m == 0:
            own[5].wait()
            for p in range(1, heads_axis):
                x_copy(p).start()
            for p in range(1, heads_axis):
                plane(z, p).start()

    acc[...] = jnp.zeros_like(acc)
    at_row = lax.broadcasted_iota(jnp.int32, (length, length), 0)
    at_col = lax.broadcasted_iota(jnp.int32, (length, length), 1)
    for h in range(heads):
        steps = ld_ref[h : h + 1, :]
        run_col = jnp.sum(jnp.where(at_row >= at_col, steps, 0.0), axis=1, keepdims=True)
        run_row = jnp.sum(jnp.where(at_row == at_col, run_col, 0.0), axis=0, keepdims=True)
        runs[h] = jnp.broadcast_to(run_col, (length, HEAD_DIM))
        decay[h] = jnp.exp(jnp.where(at_row >= at_col, run_col - run_row, -jnp.inf))
    def frames_landed():
        for p in range(1, heads_axis):
            at = peer(p)
            ref = x.at[pl.ds(pl.multiple_of(at * frames_here, frames_here), frames_here), :]
            remote(ref, ref, x_send.at[p], x_recv.at[at], sibling).wait_recv()

    def lap(d, _):
        for m in order:
            pass_on(m, d)
        return 0

    lax.fori_loop(1, zs - 1, lap, 0)
    frames_landed()

    def products(d, _):
        for m in range(1, kinds):
            project(m, d)
        plane_pass_on(d)
        return 0

    lax.fori_loop(0, zs - 1, products, 0)
    for m in (1, 2):
        pass_on(m, zs - 1)
        project(m, zs - 1)

    def columns_of(h):
        return slice(h * HEAD_DIM, (h + 1) * HEAD_DIM)

    def first_copy(h):
        return remote(sown.at[h], sprev.at[h], s_send.at[h], s_recv.at[h], sibling)

    def next_copy(h):
        return remote(rout.at[h], rin.at[h], r_send.at[h], r_recv.at[h], (tm + 2, hd))

    def share_copy(h):
        return remote(rin.at[h], rin.at[h], rs_send.at[h], r_recv.at[h], sibling)

    def state_step(h):
        prior = jnp.exp(sprev[h, HEAD_DIM : HEAD_DIM + 1, :]) * rin[h] + sprev[h, :HEAD_DIM, :]
        rout[h] = jnp.exp(sown[h, HEAD_DIM : HEAD_DIM + 1, :]) * prior + sown[h, :HEAD_DIM, :]
        return prior

    @pl.when(z == 0)
    def _():
        rin[...] = jnp.zeros_like(rin)

    for h in range(heads):
        run = runs[h]
        last = run[length - 1 :, :]
        key = acc[0, :, columns_of(h)].astype(BF16)
        value = acc[1, :, columns_of(h)].astype(BF16)
        scaled = (key.astype(F32) * jnp.exp(last - run)).astype(BF16)
        sown[h, :HEAD_DIM, :] = lax.dot_general(
            scaled, value, (((0,), (0,)), ((), ())), preferred_element_type=F32
        )
        sown[h, HEAD_DIM:, :] = jnp.broadcast_to(last, (8, HEAD_DIM))

        @pl.when(c == 0)
        def _():
            first_copy(h).start()

    @pl.when(jnp.logical_and(c == 1, z == 0))
    def _():
        for h in range(heads):
            first_copy(h).wait_recv()
            state_step(h)
            next_copy(h).start()

    pass_on(0, zs - 1)
    pass_on(3, zs - 1)
    project(3, zs - 1)
    for h in range(heads):
        query = acc[2, :, columns_of(h)].astype(BF16)
        key = acc[0, :, columns_of(h)].astype(BF16)
        value = acc[1, :, columns_of(h)].astype(BF16)
        scores = lax.dot_general(query, key, (((1,), (1,)), ((), ())), preferred_element_type=F32)
        weights = (scores * decay[h]).astype(BF16)
        ret[:, columns_of(h)] = jnp.dot(weights, value, preferred_element_type=F32)
    pass_on(4, zs - 1)

    @pl.when(jnp.logical_and(c == 1, z > 0))
    def _():
        for h in range(heads):
            first_copy(h).wait_recv()
        for h in range(heads):
            next_copy(h).wait_recv()
            state_step(h)

            @pl.when(z < zs - 1)
            def _():
                next_copy(h).start()

            share_copy(h).start()

    @pl.when(jnp.logical_and(c == 0, z > 0))
    def _():
        for h in range(heads):
            share_copy(h).wait_recv()

    for h in range(heads):

        @pl.when(c == 1)
        def _():
            rout[heads + h] = (
                jnp.exp(sprev[h, HEAD_DIM : HEAD_DIM + 1, :]) * rin[h] + sprev[h, :HEAD_DIM, :]
            )

        @pl.when(c == 0)
        def _():
            rout[heads + h] = rin[h]

        query = acc[2, :, columns_of(h)].astype(BF16)
        lifted = query.astype(F32) * jnp.exp(runs[h])
        both_parts = ret[:, columns_of(h)] + jnp.dot(
            lifted, rout[heads + h], preferred_element_type=F32, precision=lax.Precision.HIGHEST
        )
        centred = both_parts - jnp.mean(both_parts, axis=1, keepdims=True)
        spread = jnp.mean(centred * centred, axis=1, keepdims=True)
        ret[:, columns_of(h)] = centred * lax.rsqrt(spread + 1e-05)

    def rows_of(at):
        return pl.ds(pl.multiple_of(at * frames_here, frames_here), frames_here)

    def g_copy(p, part):
        at, out = peer(p), gate_columns(part)
        return remote(
            gated.at[rows_of(at), out], owned.at[hd, :, out],
            g_send.at[p, part], g_recv.at[hd, part], (tm, at),
        )

    def gate_rows(at, part):
        out = gate_columns(part)
        gate = acc[3, rows_of(at), out]
        return (gate / (1.0 + jnp.exp(-gate)) * ret[rows_of(at), out]).astype(BF16)

    for part in range(parts):
        if part > 0:
            pass_on(4 + part, zs - 1)
        project(4 + part, zs - 1)
        for p in range(1, heads_axis):
            gated[rows_of(peer(p)), gate_columns(part)] = gate_rows(peer(p), part)
            g_copy(p, part).start()
        owned[hd, :, gate_columns(part)] = gate_rows(hd, part)
        if part == 0:
            plane_pass_on(zs - 1)

    def all_out(zo, _):
        for at in range(heads_axis):
            out_landed(at, 2 * zo + 1 - c)
        return 0

    lax.fori_loop(0, zs, all_out, 0)
    wide = wo_ref.shape[1]
    for part in range(parts):
        out = gate_columns(part)
        for p in range(1, heads_axis):
            ref = owned.at[peer(p), :, out]
            remote(ref, ref, g_send.at[p, part], g_recv.at[peer(p), part], sibling).wait_recv()

        def finish(t, _):
            here = pl.ds(pl.multiple_of(t * wide, wide), wide)
            piece = jnp.zeros((frames_here, wide), F32) if part == 0 else total[:, here]
            for at in range(heads_axis):
                piece += jnp.dot(owned[at, :, out], wo[at, t, out, :], preferred_element_type=F32)
            if part < parts - 1:
                total[:, here] = piece
            else:
                out_ref[:, here] = piece.astype(BF16)
            return 0

        lax.fori_loop(0, tms, finish, 0)

    for p in range(1, heads_axis):
        x_copy(p).wait_send()
        for part in range(parts):
            g_copy(p, part).wait_send()

    @pl.when(c == 0)
    def _():
        for h in range(heads):
            first_copy(h).wait_send()

    @pl.when(c == 1)
    def _():
        for h in range(heads):

            @pl.when(z < zs - 1)
            def _():
                next_copy(h).wait_send()

            @pl.when(z > 0)
            def _():
                share_copy(h).wait_send()

    def drain(zo, _):
        for m in range(kinds):
            across(m, zo).wait_send()

            @pl.when(jnp.logical_and(zo <= z, z < zs - 1))
            def _():
                along(m, zo, 0).wait_send()

            @pl.when(jnp.logical_and(zo >= z, z > 0))
            def _():
                along(m, zo, 1).wait_send()

        for p in range(1, heads_axis):
            plane(zo, p).wait_send()
            plane_across(zo, p).wait_send()
        return 0

    lax.fori_loop(0, zs, drain, 0)


def solution(mesh):
    tms, heads_axis = mesh.shape["tm"], mesh.shape["head"]
    zs = tms // 2

    def shards(frames, log_decay, w_query, w_key, w_value, w_gate, w_out):
        here, model = frames.shape
        rows, width = w_query.shape
        length, heads = log_decay.shape
        vmem = pl.BlockSpec(memory_space=pltpu.VMEM)
        hbm = pl.BlockSpec(memory_space=pltpu.HBM)
        dma = pltpu.SemaphoreType.DMA
        return pl.pallas_call(
            functools.partial(kernel, tms, heads_axis),
            out_shape=jax.ShapeDtypeStruct((here, model), BF16),
            in_specs=[hbm, vmem] + [hbm] * 5,
            out_specs=vmem,
            scratch_shapes=[
                pltpu.VMEM((here, model), F32),
                dma((6,)),
                pltpu.VMEM((length, model), BF16),
                pltpu.VMEM((4, tms, rows, width), BF16),
                pltpu.VMEM((heads_axis, tms) + w_out.shape, BF16),
                pltpu.VMEM((4, length, width), F32),
                pltpu.VMEM((heads, length, length), F32),
                pltpu.VMEM((heads, length, HEAD_DIM), F32),
                pltpu.VMEM((heads, HEAD_DIM + 8, HEAD_DIM), F32),
                pltpu.VMEM((heads, HEAD_DIM + 8, HEAD_DIM), F32),
                pltpu.VMEM((heads, HEAD_DIM, HEAD_DIM), F32),
                pltpu.VMEM((2 * heads, HEAD_DIM, HEAD_DIM), F32),
                pltpu.VMEM((length, width), F32),
                pltpu.VMEM((length, width), BF16),
                pltpu.VMEM((heads_axis, here, width), BF16),
                dma((heads_axis,)),
                dma((heads_axis,)),
                dma((6, zs, 3)),
                dma((5, tms)),
                dma((heads_axis, tms)),
                dma((zs, heads_axis)),
                dma((zs, heads_axis)),
                dma((heads,)),
                dma((heads,)),
                dma((heads,)),
                dma((heads,)),
                dma((heads,)),
                dma((heads_axis, 2)),
                dma((heads_axis, 2)),
            ],
            compiler_params=pltpu.CompilerParams(
                collective_id=0, has_side_effects=True, vmem_limit_bytes=62 * 2**20
            ),
        )(frames, log_decay.T, w_key, w_value, w_query, w_gate, w_out)

    return jax.shard_map(
        shards,
        mesh=mesh,
        in_specs=(
            P(("tm", "head"), None),
            P("tm", "head"),
            P("tm", "head"),
            P("tm", "head"),
            P("tm", "head"),
            P("tm", "head"),
            P("head", "tm"),
        ),
        out_specs=P(("tm", "head"), None),
        check_vma=False,
    )
```

```python
import functools

import jax
import jax.numpy as jnp
from jax import lax
from jax.experimental import pallas as pl
from jax.experimental.pallas import tpu as pltpu
from jax.sharding import PartitionSpec as P

HEAD_DIM = 128
MESH = pl.DeviceIdType.MESH
F32 = jnp.float32
BF16 = jnp.bfloat16


def kernel(
    tms, heads_axis, x_ref, ld_ref, wk_ref, wv_ref, wq_ref, wg_ref, wo_ref, out_ref,
    total, in_sem, x, w, wo, acc, decay, runs, sown, sprev, rin, rnext, rout, ret, gated, owned,
    x_send, x_recv, w_send, w_recv, o_recv, oxy_send, osib_send,
    s_send, s_recv, r_send, r_recv, rs_send, g_send, g_recv,
):
    zs = tms // 2
    tm, hd = lax.axis_index("tm"), lax.axis_index("head")
    z, c = lax.div(tm, 2), lax.rem(tm, 2)
    sibling = (2 * z + 1 - c, hd)
    rows = wk_ref.shape[0]
    width = wk_ref.shape[1]
    frames_here = x_ref.shape[0]
    length = frames_here * heads_axis
    heads = width // HEAD_DIM
    parts = 2 if heads % 2 == 0 else 1
    part_width = width // parts
    kinds = 4 + parts
    order = (1, 2, 0) + tuple(range(3, kinds))

    def gate_columns(part):
        return slice(part * part_width, (part + 1) * part_width)

    def peer(p):
        return lax.rem(hd + p, heads_axis)

    def remote(ref_from, ref_to, send, recv, device):
        return pltpu.make_async_remote_copy(
            src_ref=ref_from, dst_ref=ref_to, send_sem=send, recv_sem=recv,
            device_id=device, device_id_type=MESH,
        )

    def slot(m, position):
        if m == 0:
            return wo.at[hd, position], o_recv.at[hd, position]
        if m >= 4:
            return w.at[3, position, :, gate_columns(m - 4)], w_recv.at[m - 1, position]
        return w.at[m - 1, position], w_recv.at[m - 1, position]

    def along(m, zo, side):
        ref, recv = slot(m, 2 * zo + c)
        to = z + 1 - 2 * side
        return remote(ref, ref, w_send.at[m, zo, side], recv, (2 * to + c, hd))

    def across(m, zo):
        ref, recv = slot(m, 2 * zo + c)
        return remote(ref, ref, w_send.at[m, zo, 2], recv, sibling)

    def landed(m, position):
        ref, recv = slot(m, position)
        remote(ref, ref, w_send.at[m, 0, 2], recv, sibling).wait_recv()

    def plane(zo, p):
        ref = wo.at[hd, 2 * zo + c]
        return remote(ref, ref, oxy_send.at[zo, p], o_recv.at[hd, 2 * zo + c], (tm, peer(p)))

    def plane_across(zo, p):
        at = peer(p)
        ref = wo.at[at, 2 * zo + c]
        return remote(ref, ref, osib_send.at[zo, p], o_recv.at[at, 2 * zo + c], sibling)

    def out_landed(at, position):
        ref = wo.at[at, position]
        remote(ref, ref, osib_send.at[0, 0], o_recv.at[at, position], sibling).wait_recv()

    def both(d, body):
        def one(side, _):
            zo = z - d + 2 * d * side
            first = jnp.logical_or(side == 0, d > 0)

            @pl.when(jnp.logical_and(first, jnp.logical_and(zo >= 0, zo < zs)))
            def _():
                body(zo, side)

            return 0

        lax.fori_loop(0, 2, one, 0)

    def pass_on(m, d):
        def body(zo, side):
            landed(m, 2 * zo + c)
            to = z + 1 - 2 * side

            @pl.when(jnp.logical_and(to >= 0, to < zs))
            def _():
                along(m, zo, side).start()

            across(m, zo).start()
            if m == 0:
                for p in range(1, heads_axis):
                    plane(zo, p).start()

        both(d, body)

    def project(m, d):
        def body(zo, side):
            landed(m, 2 * zo + 1 - c)
            columns = pl.ds(pl.multiple_of(zo * (2 * rows), 2 * rows), 2 * rows)
            out = gate_columns(m - 4) if m >= 4 else slice(0, width)
            at = min(m - 1, 3)
            block = w[at, pl.ds(2 * zo, 2), :, out].reshape(2 * rows, out.stop - out.start)
            acc[at, :, out] += jnp.dot(x[:, columns], block, preferred_element_type=F32)

        both(d, body)

    def plane_pass_on(d):
        def body(zo, side):
            for p in range(1, heads_axis):
                out_landed(peer(p), 2 * zo + c)
                plane_across(zo, p).start()

        both(d, body)

    barrier = pltpu.get_barrier_semaphore()
    pl.semaphore_signal(barrier, inc=1, device_id=sibling, device_id_type=MESH)
    for p in range(1, heads_axis):
        pl.semaphore_signal(barrier, inc=1, device_id=(tm, peer(p)), device_id_type=MESH)

    @pl.when(z > 0)
    def _():
        pl.semaphore_signal(barrier, inc=1, device_id=(tm - 2, hd), device_id_type=MESH)

    @pl.when(z < zs - 1)
    def _():
        pl.semaphore_signal(barrier, inc=1, device_id=(tm + 2, hd), device_id_type=MESH)

    here = pl.ds(pl.multiple_of(hd * frames_here, frames_here), frames_here)
    own = [
        pltpu.make_async_copy(wo_ref, wo.at[hd, tm], in_sem.at[0]),
        pltpu.make_async_copy(wk_ref, w.at[0, tm], in_sem.at[1]),
        pltpu.make_async_copy(wv_ref, w.at[1, tm], in_sem.at[2]),
        pltpu.make_async_copy(wq_ref, w.at[2, tm], in_sem.at[3]),
        pltpu.make_async_copy(wg_ref, w.at[3, tm], in_sem.at[4]),
        pltpu.make_async_copy(x_ref, x.at[here, :], in_sem.at[5]),
    ]
    for copy in own:
        copy.start()
    neighbours = (z > 0).astype(jnp.int32) + (z < zs - 1).astype(jnp.int32)
    pl.semaphore_wait(barrier, heads_axis + neighbours)

    def x_copy(p):
        return remote(x.at[here, :], x.at[here, :], x_send.at[p], x_recv.at[hd], (tm, peer(p)))

    for m in order:
        if m < 5:
            own[m].wait()

        @pl.when(z < zs - 1)
        def _():
            along(m, z, 0).start()

        @pl.when(z > 0)
        def _():
            along(m, z, 1).start()

        across(m, z).start()
        if m == 0:
            own[5].wait()
            for p in range(1, heads_axis):
                x_copy(p).start()
            for p in range(1, heads_axis):
                plane(z, p).start()

    acc[...] = jnp.zeros_like(acc)
    at_row = lax.broadcasted_iota(jnp.int32, (length, length), 0)
    at_col = lax.broadcasted_iota(jnp.int32, (length, length), 1)
    for h in range(heads):
        steps = ld_ref[h : h + 1, :]
        run_col = jnp.sum(jnp.where(at_row >= at_col, steps, 0.0), axis=1, keepdims=True)
        run_row = jnp.sum(jnp.where(at_row == at_col, run_col, 0.0), axis=0, keepdims=True)
        runs[h] = jnp.broadcast_to(run_col, (length, HEAD_DIM))
        decay[h] = jnp.exp(jnp.where(at_row >= at_col, run_col - run_row, -jnp.inf))
    def frames_landed():
        for p in range(1, heads_axis):
            at = peer(p)
            ref = x.at[pl.ds(pl.multiple_of(at * frames_here, frames_here), frames_here), :]
            remote(ref, ref, x_send.at[p], x_recv.at[at], sibling).wait_recv()

    def lap(d, _):
        for m in order:
            pass_on(m, d)
        return 0

    lax.fori_loop(1, zs - 1, lap, 0)
    frames_landed()

    def products(d, _):
        for m in range(1, kinds):
            project(m, d)
        plane_pass_on(d)
        return 0

    lax.fori_loop(0, zs - 1, products, 0)
    for m in (1, 2):
        pass_on(m, zs - 1)
        project(m, zs - 1)

    def columns_of(h):
        return slice(h * HEAD_DIM, (h + 1) * HEAD_DIM)

    def first_copy(h):
        return remote(sown.at[h], sprev.at[h], s_send.at[h], s_recv.at[h], sibling)

    def next_copy(h):
        return remote(rnext.at[h], rin.at[h], r_send.at[h], r_recv.at[h], (tm + 2, hd))

    def share_copy(h):
        return remote(rin.at[h], rin.at[h], rs_send.at[h], r_recv.at[h], sibling)

    def state_step(h):
        prior = jnp.exp(sprev[h, HEAD_DIM : HEAD_DIM + 1, :]) * rin[h].astype(F32) + sprev[h, :HEAD_DIM, :]
        later = jnp.exp(sown[h, HEAD_DIM : HEAD_DIM + 1, :]) * prior + sown[h, :HEAD_DIM, :]
        rnext[h] = later.astype(BF16)

    @pl.when(z == 0)
    def _():
        rin[...] = jnp.zeros_like(rin)

    for h in range(heads):
        run = runs[h]
        last = run[length - 1 :, :]
        key = acc[0, :, columns_of(h)].astype(BF16)
        value = acc[1, :, columns_of(h)].astype(BF16)
        scaled = (key.astype(F32) * jnp.exp(last - run)).astype(BF16)
        sown[h, :HEAD_DIM, :] = lax.dot_general(
            scaled, value, (((0,), (0,)), ((), ())), preferred_element_type=F32
        )
        sown[h, HEAD_DIM:, :] = jnp.broadcast_to(last, (8, HEAD_DIM))

        @pl.when(c == 0)
        def _():
            first_copy(h).start()

    @pl.when(jnp.logical_and(c == 1, z == 0))
    def _():
        for h in range(heads):
            first_copy(h).wait_recv()
            state_step(h)
            next_copy(h).start()

    pass_on(0, zs - 1)
    pass_on(3, zs - 1)
    project(3, zs - 1)
    for h in range(heads):
        query = acc[2, :, columns_of(h)].astype(BF16)
        key = acc[0, :, columns_of(h)].astype(BF16)
        value = acc[1, :, columns_of(h)].astype(BF16)
        scores = lax.dot_general(query, key, (((1,), (1,)), ((), ())), preferred_element_type=F32)
        weights = (scores * decay[h]).astype(BF16)
        ret[:, columns_of(h)] = jnp.dot(weights, value, preferred_element_type=F32)
    pass_on(4, zs - 1)

    @pl.when(jnp.logical_and(c == 1, z > 0))
    def _():
        for h in range(heads):
            first_copy(h).wait_recv()
        for h in range(heads):
            next_copy(h).wait_recv()
            state_step(h)

            @pl.when(z < zs - 1)
            def _():
                next_copy(h).start()

            share_copy(h).start()

    @pl.when(jnp.logical_and(c == 0, z > 0))
    def _():
        for h in range(heads):
            share_copy(h).wait_recv()

    for h in range(heads):

        @pl.when(c == 1)
        def _():
            rout[h] = (
                jnp.exp(sprev[h, HEAD_DIM : HEAD_DIM + 1, :]) * rin[h].astype(F32) + sprev[h, :HEAD_DIM, :]
            )

        @pl.when(c == 0)
        def _():
            rout[h] = rin[h].astype(F32)

        query = acc[2, :, columns_of(h)].astype(BF16)
        lifted = query.astype(F32) * jnp.exp(runs[h])
        both_parts = ret[:, columns_of(h)] + jnp.dot(
            lifted, rout[h], preferred_element_type=F32, precision=lax.Precision.HIGHEST
        )
        centred = both_parts - jnp.mean(both_parts, axis=1, keepdims=True)
        spread = jnp.mean(centred * centred, axis=1, keepdims=True)
        ret[:, columns_of(h)] = centred * lax.rsqrt(spread + 1e-05)

    def rows_of(at):
        return pl.ds(pl.multiple_of(at * frames_here, frames_here), frames_here)

    def g_copy(p, part):
        at, out = peer(p), gate_columns(part)
        return remote(
            gated.at[rows_of(at), out], owned.at[hd, :, out],
            g_send.at[p, part], g_recv.at[hd, part], (tm, at),
        )

    def gate_rows(at, part):
        out = gate_columns(part)
        gate = acc[3, rows_of(at), out]
        return (gate / (1.0 + jnp.exp(-gate)) * ret[rows_of(at), out]).astype(BF16)

    for part in range(parts):
        if part > 0:
            pass_on(4 + part, zs - 1)
        project(4 + part, zs - 1)
        for p in range(1, heads_axis):
            gated[rows_of(peer(p)), gate_columns(part)] = gate_rows(peer(p), part)
            g_copy(p, part).start()
        owned[hd, :, gate_columns(part)] = gate_rows(hd, part)
        if part == 0:
            plane_pass_on(zs - 1)

    def all_out(zo, _):
        for at in range(heads_axis):
            out_landed(at, 2 * zo + 1 - c)
        return 0

    lax.fori_loop(0, zs, all_out, 0)
    wide = wo_ref.shape[1]
    for part in range(parts):
        out = gate_columns(part)
        for p in range(1, heads_axis):
            ref = owned.at[peer(p), :, out]
            remote(ref, ref, g_send.at[p, part], g_recv.at[peer(p), part], sibling).wait_recv()

        def finish(t, _):
            here = pl.ds(pl.multiple_of(t * wide, wide), wide)
            piece = jnp.zeros((frames_here, wide), F32) if part == 0 else total[:, here]
            for at in range(heads_axis):
                piece += jnp.dot(owned[at, :, out], wo[at, t, out, :], preferred_element_type=F32)
            if part < parts - 1:
                total[:, here] = piece
            else:
                out_ref[:, here] = piece.astype(BF16)
            return 0

        lax.fori_loop(0, tms, finish, 0)

    for p in range(1, heads_axis):
        x_copy(p).wait_send()
        for part in range(parts):
            g_copy(p, part).wait_send()

    @pl.when(c == 0)
    def _():
        for h in range(heads):
            first_copy(h).wait_send()

    @pl.when(c == 1)
    def _():
        for h in range(heads):

            @pl.when(z < zs - 1)
            def _():
                next_copy(h).wait_send()

            @pl.when(z > 0)
            def _():
                share_copy(h).wait_send()

    def drain(zo, _):
        for m in range(kinds):
            across(m, zo).wait_send()

            @pl.when(jnp.logical_and(zo <= z, z < zs - 1))
            def _():
                along(m, zo, 0).wait_send()

            @pl.when(jnp.logical_and(zo >= z, z > 0))
            def _():
                along(m, zo, 1).wait_send()

        for p in range(1, heads_axis):
            plane(zo, p).wait_send()
            plane_across(zo, p).wait_send()
        return 0

    lax.fori_loop(0, zs, drain, 0)


def solution(mesh):
    tms, heads_axis = mesh.shape["tm"], mesh.shape["head"]
    zs = tms // 2

    def shards(frames, log_decay, w_query, w_key, w_value, w_gate, w_out):
        here, model = frames.shape
        rows, width = w_query.shape
        length, heads = log_decay.shape
        vmem = pl.BlockSpec(memory_space=pltpu.VMEM)
        hbm = pl.BlockSpec(memory_space=pltpu.HBM)
        dma = pltpu.SemaphoreType.DMA
        return pl.pallas_call(
            functools.partial(kernel, tms, heads_axis),
            out_shape=jax.ShapeDtypeStruct((here, model), BF16),
            in_specs=[hbm, vmem] + [hbm] * 5,
            out_specs=vmem,
            scratch_shapes=[
                pltpu.VMEM((here, model), F32),
                dma((6,)),
                pltpu.VMEM((length, model), BF16),
                pltpu.VMEM((4, tms, rows, width), BF16),
                pltpu.VMEM((heads_axis, tms) + w_out.shape, BF16),
                pltpu.VMEM((4, length, width), F32),
                pltpu.VMEM((heads, length, length), F32),
                pltpu.VMEM((heads, length, HEAD_DIM), F32),
                pltpu.VMEM((heads, HEAD_DIM + 8, HEAD_DIM), F32),
                pltpu.VMEM((heads, HEAD_DIM + 8, HEAD_DIM), F32),
                pltpu.VMEM((heads, HEAD_DIM, HEAD_DIM), BF16),
                pltpu.VMEM((heads, HEAD_DIM, HEAD_DIM), BF16),
                pltpu.VMEM((heads, HEAD_DIM, HEAD_DIM), F32),
                pltpu.VMEM((length, width), F32),
                pltpu.VMEM((length, width), BF16),
                pltpu.VMEM((heads_axis, here, width), BF16),
                dma((heads_axis,)),
                dma((heads_axis,)),
                dma((6, zs, 3)),
                dma((5, tms)),
                dma((heads_axis, tms)),
                dma((zs, heads_axis)),
                dma((zs, heads_axis)),
                dma((heads,)),
                dma((heads,)),
                dma((heads,)),
                dma((heads,)),
                dma((heads,)),
                dma((heads_axis, 2)),
                dma((heads_axis, 2)),
            ],
            compiler_params=pltpu.CompilerParams(
                collective_id=0, has_side_effects=True, vmem_limit_bytes=62 * 2**20
            ),
        )(frames, log_decay.T, w_key, w_value, w_query, w_gate, w_out)

    return jax.shard_map(
        shards,
        mesh=mesh,
        in_specs=(
            P(("tm", "head"), None),
            P("tm", "head"),
            P("tm", "head"),
            P("tm", "head"),
            P("tm", "head"),
            P("tm", "head"),
            P("head", "tm"),
        ),
        out_specs=P(("tm", "head"), None),
        check_vma=False,
    )
```
